256 devices in a mesh: dom: 16 (over x, y), fsdp: 16 (over z, core).
Axes of the slice: x: 4, y: 4, z: 8, core: 2. Of those that a mesh axis runs over, the one named last changes fastest.
Arguments:
- tokens: bfloat16 [16, 768, 4096], P('dom', 'fsdp'), may hold values from -8 to 8
- hidden_grad: bfloat16 [16, 768, 8192], P('dom', None, 'fsdp'), may hold values from -2.5 to 2.5
- gate_weight: bfloat16 [4096, 8192], P('dom', 'fsdp'), may hold values from -0.09375 to 0.09375
- up_weight: bfloat16 [4096, 8192], P('dom', 'fsdp'), may hold values from -0.09375 to 0.09375
- counts: int32 [16], replicated, may hold values from 1 to 8
Outputs:
- mix_gate: float32 [4096, 8192], P('dom', 'fsdp')
- mix_up: float32 [4096, 8192], P('dom', 'fsdp')
- alpha: float32 [16], replicated
The draws below stay inside these ranges and needn't reach their ends.
All inputs are finite; a program needn't handle non-finite values.
Results may differ from the reference program's by a relative error of at most 0.0034.
Values may be sent and summed in bfloat16 or wider, within the bound.
A program may use at most 128 MiB of HBM per device.

```python
import jax
import jax.numpy as jnp
from jax import lax

D = 4096
HID = 8192
TOKENS_DOM = 768
DOMAINS = 16
N_DOM = 16


def blend_domains(key, width, magnitude, column_spread, limit):
    coef_key, shared_key, own_key = jax.random.split(key, 3)
    column_key = jax.random.fold_in(key, 17)
    weight_shared = jax.random.uniform(coef_key, (DOMAINS, 1, 1), jnp.float32, 0.6, 0.98)
    column_normal = jax.random.normal(column_key, (DOMAINS, 1, width), jnp.float32)
    column_scale = jnp.exp(column_spread * column_normal - column_spread * column_spread)
    shared = jnp.clip(jax.random.normal(shared_key, (1, TOKENS_DOM, width), jnp.float32), -4.0, 4.0)
    own_part = jnp.clip(jax.random.normal(own_key, (DOMAINS, TOKENS_DOM, width), jnp.float32), -4.0, 4.0)
    blended = weight_shared * shared + jnp.sqrt(1.0 - weight_shared * weight_shared) * own_part
    values = magnitude * blended * column_scale
    return jnp.clip(values, -limit, limit).astype(jnp.bfloat16)


def draw_tokens(key, part):
    key = jax.random.fold_in(key, 5)
    return blend_domains(key, D, 1.0, 0.0, 8.0)


def draw_hidden_grad(key, part):
    key = jax.random.fold_in(key, 9)
    return blend_domains(key, HID, 0.1, 1.2, 2.5)


def plant(array, stream_key, low, largest):
    shape = array.shape
    spot = [jax.random.randint(jax.random.fold_in(stream_key, axis), (), 0, shape[axis]) for axis in range(len(shape))]
    array = array.at[tuple(spot)].set(low)
    longest = shape.index(max(shape))
    spot[longest] = (spot[longest] + 1) % shape[longest]
    return array.at[tuple(spot)].set(largest)


def block_scale(key, dims, cuts, smallest, largest):
    def one(dim, blocks):
        steps = jax.random.uniform(jax.random.fold_in(jax.random.fold_in(key, 6), dim), (blocks,), jnp.float32, smallest / len(cuts), largest / len(cuts))
        return jnp.repeat(jnp.exp(steps), dims[dim] // blocks).reshape((-1,) + (1,) * (len(dims) - dim - 1))

    loudness = one(*cuts[0])
    for cut in cuts[1:]:
        loudness = loudness * one(*cut)
    return loudness


def centred(stream_key, extent, scale, reach, cuts=(), kind=jnp.bfloat16):
    gain = block_scale(stream_key, extent, cuts, -0.22, 0.18) if cuts else 1.0
    array = jax.random.normal(stream_key, extent, jnp.float32) * scale * gain
    return jnp.minimum(jnp.maximum(array, -reach), reach).astype(kind)


def setup_inputs(seed: int = 0) -> dict:
    arg_keys = jax.random.split(jax.random.key(seed), 6)
    return {
        "tokens": draw_tokens(jax.random.fold_in(arg_keys[5], 71), 0),
        "hidden_grad": draw_hidden_grad(jax.random.fold_in(arg_keys[5], 71), 0),
        "gate_weight": centred(arg_keys[2], (D, HID), D ** -0.5, 0.09375, ((0, 16), (1, 16))),
        "up_weight": centred(arg_keys[3], (D, HID), D ** -0.5, 0.09375, ((0, 16), (1, 16))),
        "counts": plant(jax.random.randint(arg_keys[4], (DOMAINS,), 1, 9), jax.random.fold_in(arg_keys[4], 1), 1, 8).astype(jnp.int32),
    }


STEP_SIZE = 4.0
EPS = 1e-06

def domain_weights(gram, counts):
    prior = counts.astype(jnp.float32) / jnp.sum(counts.astype(jnp.float32))
    toward = jnp.dot(gram, prior, precision=lax.Precision.HIGHEST)
    spread = jnp.dot(prior, toward, precision=lax.Precision.HIGHEST)
    cosine = toward / jnp.sqrt((jnp.diagonal(gram) + EPS) * (spread + EPS))
    scaled = prior * jnp.exp(STEP_SIZE * cosine)
    return scaled / jnp.sum(scaled)

def rounded(value):
    return lax.optimization_barrier(value.astype(jnp.bfloat16)).astype(jnp.float32)

def reference(tokens, hidden_grad, gate_weight, up_weight, counts):
    features = tokens.astype(jnp.float32)
    gate_pre = jnp.einsum('jtd,dh->jth', features, gate_weight.astype(jnp.float32), precision=lax.Precision.HIGHEST)
    up_pre = jnp.einsum('jtd,dh->jth', features, up_weight.astype(jnp.float32), precision=lax.Precision.HIGHEST)
    sig_gate = jax.nn.sigmoid(gate_pre)
    upstream = hidden_grad.astype(jnp.float32)
    gate_act = rounded(upstream * up_pre * sig_gate * (1.0 + gate_pre * (1.0 - sig_gate)))
    up_act = rounded(upstream * gate_pre * sig_gate)
    block = D // N_DOM

    def grads(offset):
        feat_block = lax.dynamic_slice_in_dim(features, offset, block, 2)
        grad_gate = jnp.einsum('jtk,jth->jkh', feat_block, gate_act, precision=lax.Precision.HIGHEST)
        grad_up = jnp.einsum('jtk,jth->jkh', feat_block, up_act, precision=lax.Precision.HIGHEST)
        return (rounded(grad_gate), rounded(grad_up))

    def gram_part(offset):
        grad_gate, grad_up = grads(offset)
        flat_gate = grad_gate.reshape(N_DOM, -1)
        flat_up = grad_up.reshape(N_DOM, -1)
        return jnp.dot(flat_gate, flat_gate.T, precision=lax.Precision.HIGHEST) + jnp.dot(flat_up, flat_up.T, precision=lax.Precision.HIGHEST)
    offsets = jnp.arange(N_DOM, dtype=jnp.int32) * block
    gram = lax.optimization_barrier(jnp.sum(lax.map(gram_part, offsets), axis=0))
    alpha = domain_weights(gram, counts)

    def mixture(offset):
        grad_gate, grad_up = grads(offset)
        return (lax.optimization_barrier(jnp.sum(alpha[:, None, None] * grad_gate, axis=0)), lax.optimization_barrier(jnp.sum(alpha[:, None, None] * grad_up, axis=0)))
    mix_gate, mix_up = lax.map(mixture, offsets)
    return (mix_gate.reshape(D, HID), mix_up.reshape(D, HID), alpha)
```

```python
import functools

import jax
import jax.numpy as jnp
from jax import lax
from jax.experimental import pallas as pl
from jax.experimental.pallas import tpu as pltpu
from jax.sharding import PartitionSpec as P

STEP_SIZE = 4.0
EPS = 1e-06
MESH = pl.DeviceIdType.MESH

SIDE = 4
N_DOM = 16
N_FSDP = 16
CHUNKS = 4
LANES = 128
ROWS = 256
TOK = 48
TOKENS = 768
D = 4096
HALF_D = D // 2


def wrap(i, n):
    return lax.rem(i + n, n)


def remote(src, dst, ss, rs, **where):
    return pltpu.make_async_remote_copy(
        src_ref=src, dst_ref=dst, send_sem=ss, recv_sem=rs, device_id=where, device_id_type=MESH
    )


def kernel(
    tok_ref, hg_ref, gw_ref, uw_ref, cnt_ref,
    og_ref, ou_ref, oa_ref,
    tokens, tokens_t, weights, grads, stack, acts, mean, scale, part, part2, ar1, ar2,
    rs_s, rs_r, sb_s, sb_r, w1_s, w1_r, w2_s, w2_r, g_s, g_r, a1_s, a1_r, a2_s, a2_r,
):
    me = lax.axis_index("dom")
    x, y = me // SIDE, lax.rem(me, SIDE)
    f = lax.axis_index("fsdp")
    z, core = f // 2, lax.rem(f, 2)
    way = 1 - 2 * core
    sibling = f + way
    onward = wrap(z + way, 8) * 2 + core

    barrier = pltpu.get_barrier_semaphore()

    @pl.loop(1, N_DOM)
    def _(k):
        pl.semaphore_signal(barrier, inc=1, device_id={"dom": lax.rem(me + k, N_DOM)}, device_id_type=MESH)
        pl.semaphore_signal(barrier, inc=1, device_id={"fsdp": lax.rem(f + k, N_FSDP)}, device_id_type=MESH)

    pl.semaphore_wait(barrier, 2 * (N_DOM - 1))

    def shard(s, c, h):
        owner = wrap(z - s * (1 - 2 * c) + 8, 8) * 2 + c
        return tokens.at[pl.ds(pl.multiple_of(owner * TOK, 16), TOK), pl.ds(h * HALF_D, HALF_D)]

    def ring(s, h):
        src = tok_ref.at[0, :, pl.ds(h * HALF_D, HALF_D)] if s == 0 else shard(s, core, h)
        return remote(src, shard(s, core, h), rs_s.at[s, h], rs_r.at[s, h], fsdp=onward)

    def side(s, h):
        src = tok_ref.at[0, :, pl.ds(h * HALF_D, HALF_D)] if s == 0 else shard(s, core, h)
        return remote(src, shard(s, core, h), sb_s.at[s, h], sb_r.at[s, h], fsdp=sibling)

    def token_step(s):
        for h in range(2):
            here = shard(s, core, h)
            remote(here, here, rs_s.at[s - 1, h], rs_r.at[s - 1, h], fsdp=onward).wait_recv()
            if s < 7:
                ring(s, h).start()
            side(s, h).start()

    def block(kind, c, bx, by, lo=0, n=ROWS):
        return weights.at[kind, c, bx, by, pl.ds(lo, n)]

    def line(kind, c, off, lo=0, n=ROWS):
        if kind == 0:
            return weights.at[kind, c, :, wrap(y + off, SIDE), pl.ds(lo, n)]
        return weights.at[kind, c, wrap(x + off, SIDE), :, pl.ds(lo, n)]

    def near(axis, off):
        if axis == 0:
            return wrap(x + off, SIDE) * SIDE + y
        return x * SIDE + wrap(y + off, SIDE)

    def first(kind, c, off, lo=0, n=ROWS):
        if kind == 0:
            return block(kind, c, wrap(x + off, SIDE), y, lo, n)
        return block(kind, c, x, wrap(y + off, SIDE), lo, n)

    HALF = ROWS // 2

    def w1(kind, c, i):
        axis, to = kind, (1, -1)[i % 2]
        if i < 2:
            src_ref = (gw_ref, uw_ref)[kind]
            src = src_ref.at[:, pl.ds(pl.multiple_of(c * LANES, LANES), LANES)]
            return remote(src, first(kind, c, 0), w1_s.at[kind, c, i], w1_r.at[kind, c, i], dom=near(axis, to))
        part_ = first(kind, c, -to, (i - 2) * HALF, HALF)
        return remote(part_, part_, w1_s.at[kind, c, i], w1_r.at[kind, c, i], dom=near(axis, to))

    def w1_got(kind, c, i):
        to = (1, -1)[i % 2]
        here = first(kind, c, -to) if i < 2 else first(kind, c, 2, (i - 2) * HALF, HALF)
        remote(here, here, w1_s.at[kind, c, i], w1_r.at[kind, c, i], dom=near(kind, to)).wait_recv()

    def w2(kind, c, i):
        axis, to = 1 - kind, (1, -1)[i % 2]
        src = line(kind, c, 0) if i < 2 else line(kind, c, -to, (i - 2) * HALF, HALF)
        return remote(src, src, w2_s.at[kind, c, i], w2_r.at[kind, c, i], dom=near(axis, to))

    def w2_got(kind, c, i):
        to = (1, -1)[i % 2]
        here = line(kind, c, -to) if i < 2 else line(kind, c, 2, (i - 2) * HALF, HALF)
        remote(here, here, w2_s.at[kind, c, i], w2_r.at[kind, c, i], dom=near(1 - kind, to)).wait_recv()

    for h in range(2):
        ring(0, h).start()

    @pl.loop(0, CHUNKS)
    def _(c):
        for kind in range(2):
            for i in range(2):
                w1(kind, c, i).start()

    for h in range(2):
        side(0, h).start()
    tokens[pl.ds(pl.multiple_of(f * TOK, 16), TOK), :] = tok_ref[0]
    for c in range(CHUNKS):
        weights[0, c, x, y] = gw_ref[:, c * LANES : (c + 1) * LANES]
        weights[1, c, x, y] = uw_ref[:, c * LANES : (c + 1) * LANES]

    counts = cnt_ref[...].astype(jnp.float32)
    prior = counts / jnp.sum(counts, axis=0, keepdims=True)

    def spread_out(column):
        for j in range(N_DOM):
            scale[j] = jnp.broadcast_to(column[j : j + 1, :], (1, 2 * LANES))

    spread_out(prior)
    part[...] = jnp.zeros_like(part)

    def stage_a(c):
        for kind in range(2):
            for i in range(2):
                w1_got(kind, c, i)
                w1(kind, c, i + 2).start()

    def stage_b(c):
        for kind in range(2):
            for i in range(2, 4):
                w1_got(kind, c, i)
            for i in range(2):
                w2(kind, c, i).start()

    def stage_c(c):
        for kind in range(2):
            for i in range(2):
                w2_got(kind, c, i)
                w2(kind, c, i + 2).start()

    def stage_d(c):
        for kind in range(2):
            for i in range(2, 4):
                w2_got(kind, c, i)

    token_step(1)
    pl.loop(0, CHUNKS)(stage_a)
    token_step(2)
    pl.loop(0, CHUNKS)(stage_b)
    token_step(3)
    token_step(4)
    stage_c(0)
    token_step(5)
    token_step(6)
    stage_c(1)
    token_step(7)
    stage_c(2)

    @pl.loop(0, 8)
    def _(s):
        for h in range(2):
            here = shard(s, 1 - core, h)
            remote(here, here, sb_s.at[s, h], sb_r.at[s, h], fsdp=sibling).wait_recv()

    @pl.loop(0, D // 256)
    def _(k):
        at = pl.ds(pl.multiple_of(k * 256, 256), 256)
        tokens_t[at, :] = tokens[:, at].T

    stage_c(3)

    def target(k):
        t = 1 + lax.rem(k + 8, N_DOM - 1)
        return wrap(x + t // SIDE, SIDE) * SIDE + wrap(y + lax.rem(t, SIDE), SIDE)

    def chunk(c):
        stage_d(c)

        @pl.loop(0, TOKENS // 256)
        def _(m):
            at = pl.ds(pl.multiple_of(m * 256, 256), 256)
            w = jnp.concatenate([weights[0, c].reshape(D, LANES), weights[1, c].reshape(D, LANES)], axis=1)
            pre = jnp.dot(tokens[at, :], w, preferred_element_type=jnp.float32)
            gate, up = pre[:, :LANES], pre[:, LANES:]
            g = hg_ref[0, at, pl.ds(pl.multiple_of(c * LANES, LANES), LANES)].astype(jnp.float32)
            s = jax.nn.sigmoid(gate)
            acts[at, :LANES] = (g * up * s * (1.0 + gate * (1.0 - s))).astype(jnp.bfloat16)
            acts[at, LANES:] = (g * gate * s).astype(jnp.bfloat16)

        def block_of(t):
            rows = pl.ds(pl.multiple_of(t * ROWS, ROWS), ROWS)
            out = jnp.dot(tokens_t[rows, :], acts[...], preferred_element_type=jnp.float32)
            return out.astype(jnp.bfloat16)

        @pl.loop(1, N_DOM)
        def _(k):
            t = target(k)
            grads[c, t] = block_of(t)
            remote(grads.at[c, t], stack.at[c, me], g_s.at[c, t], g_r.at[c, me], dom=t).start()

        stack[c, me] = block_of(me)

    pl.loop(0, CHUNKS)(chunk)

    def products(c):
        @pl.loop(1, N_DOM)
        def _(k):
            j = lax.rem(me + k, N_DOM)
            here = stack.at[c, j]
            remote(here, here, g_s.at[c, j], g_r.at[c, j], dom=j).wait_recv()

        @pl.loop(0, ROWS // 32)
        def _(r):
            at = pl.ds(pl.multiple_of(r * 32, 32), 32)
            total = scale[0] * stack[c, 0, at, :].astype(jnp.float32)
            for j in range(1, N_DOM):
                total += scale[j] * stack[c, j, at, :].astype(jnp.float32)
            mean[at, :] = total

        @pl.loop(0, N_DOM)
        def _(j):
            toward = jnp.zeros((8, 2 * LANES), jnp.float32)
            own = jnp.zeros((8, 2 * LANES), jnp.float32)
            for r in range(ROWS // 32):
                at = pl.ds(r * 32, 32)
                g = stack[c, j, at, :].astype(jnp.float32)
                toward += jnp.sum((g * mean[at, :]).reshape(4, 8, 2 * LANES), axis=0)
                own += jnp.sum((g * g).reshape(4, 8, 2 * LANES), axis=0)
            toward = jnp.sum(toward, axis=0, keepdims=True)
            own = jnp.sum(own, axis=0, keepdims=True)
            part[j] += toward[:, :LANES] + toward[:, LANES:]
            part[N_DOM + j] += own[:, :LANES] + own[:, LANES:]

    pl.loop(0, CHUNKS)(products)

    ar1[me] = part[...]

    @pl.loop(1, N_DOM)
    def _(k):
        t = lax.rem(me + k, N_DOM)
        remote(part, ar1.at[me], a1_s.at[t], a1_r.at[me], dom=t).start()

    @pl.loop(1, N_DOM)
    def _(k):
        t = lax.rem(me + k, N_DOM)
        remote(part, ar1.at[t], a1_s.at[t], a1_r.at[t], dom=t).wait_recv()

    total = ar1[0]
    for j in range(1, N_DOM):
        total += ar1[j]
    part2[...] = total
    ar2[f] = total

    @pl.loop(1, N_FSDP)
    def _(k):
        t = lax.rem(f + k, N_FSDP)
        remote(part2, ar2.at[f], a2_s.at[t], a2_r.at[f], fsdp=t).start()

    @pl.loop(1, N_FSDP)
    def _(k):
        t = lax.rem(f + k, N_FSDP)
        remote(part2, ar2.at[t], a2_s.at[t], a2_r.at[t], fsdp=t).wait_recv()

    total = ar2[0]
    for j in range(1, N_FSDP):
        total += ar2[j]
    total = jnp.sum(total.reshape(2 * N_DOM, LANES), axis=1, keepdims=True)
    toward, own = total[:N_DOM], total[N_DOM:]
    spread = jnp.sum(prior * toward, axis=0, keepdims=True)
    cosine = toward / jnp.sqrt((own + EPS) * (spread + EPS))
    scaled = prior * jnp.exp(STEP_SIZE * cosine)
    alpha = scaled / jnp.sum(scaled, axis=0, keepdims=True)
    oa_ref[...] = jnp.broadcast_to(alpha, (N_DOM, LANES))
    spread_out(alpha)

    for c in range(CHUNKS):
        cols = pl.ds(c * LANES, LANES)

        @pl.loop(0, ROWS // 32)
        def _(r):
            at = pl.ds(pl.multiple_of(r * 32, 32), 32)
            mix = scale[0] * stack[c, 0, at, :].astype(jnp.float32)
            for j in range(1, N_DOM):
                mix += scale[j] * stack[c, j, at, :].astype(jnp.float32)
            og_ref[at, cols] = mix[:, :LANES]
            ou_ref[at, cols] = mix[:, LANES:]

    for h in range(2):
        for s in range(7):
            ring(s, h).wait_send()
        for s in range(8):
            side(s, h).wait_send()

    @pl.loop(0, CHUNKS)
    def _(c):
        for kind in range(2):
            for i in range(4):
                w1(kind, c, i).wait_send()
                w2(kind, c, i).wait_send()

        @pl.loop(1, N_DOM)
        def _(k):
            t = lax.rem(me + k, N_DOM)
            remote(grads.at[c, t], stack.at[c, me], g_s.at[c, t], g_r.at[c, me], dom=t).wait_send()

    @pl.loop(1, N_DOM)
    def _(k):
        t = lax.rem(me + k, N_DOM)
        remote(part, ar1.at[me], a1_s.at[t], a1_r.at[me], dom=t).wait_send()
        t = lax.rem(f + k, N_FSDP)
        remote(part2, ar2.at[f], a2_s.at[t], a2_r.at[f], fsdp=t).wait_send()


def local(tokens, hidden_grad, gate_weight, up_weight, counts):
    vmem = pl.BlockSpec(memory_space=pltpu.VMEM)
    dma = pltpu.SemaphoreType.DMA
    bf16, f32 = jnp.bfloat16, jnp.float32
    mix_gate, mix_up, alpha = pl.pallas_call(
        kernel,
        out_shape=(
            jax.ShapeDtypeStruct((ROWS, CHUNKS * LANES), f32),
            jax.ShapeDtypeStruct((ROWS, CHUNKS * LANES), f32),
            jax.ShapeDtypeStruct((N_DOM, LANES), f32),
        ),
        in_specs=[vmem] * 5,
        out_specs=(vmem,) * 3,
        scratch_shapes=[
            pltpu.VMEM((TOKENS, D), bf16),
            pltpu.VMEM((D, TOKENS), bf16),
            pltpu.VMEM((2, CHUNKS, SIDE, SIDE, ROWS, LANES), bf16),
            pltpu.VMEM((CHUNKS, N_DOM, ROWS, 2 * LANES), bf16),
            pltpu.VMEM((CHUNKS, N_DOM, ROWS, 2 * LANES), bf16),
            pltpu.VMEM((TOKENS, 2 * LANES), bf16),
            pltpu.VMEM((ROWS, 2 * LANES), f32),
            pltpu.VMEM((N_DOM, 1, 2 * LANES), f32),
            pltpu.VMEM((2 * N_DOM, 1, LANES), f32),
            pltpu.VMEM((2 * N_DOM, 1, LANES), f32),
            pltpu.VMEM((N_DOM, 2 * N_DOM, 1, LANES), f32),
            pltpu.VMEM((N_FSDP, 2 * N_DOM, 1, LANES), f32),
            dma((7, 2)), dma((7, 2)), dma((8, 2)), dma((8, 2)),
            dma((2, CHUNKS, 4)), dma((2, CHUNKS, 4)), dma((2, CHUNKS, 4)), dma((2, CHUNKS, 4)),
            dma((CHUNKS, N_DOM)), dma((CHUNKS, N_DOM)),
            dma((N_DOM,)), dma((N_DOM,)), dma((N_FSDP,)), dma((N_FSDP,)),
        ],
        compiler_params=pltpu.CompilerParams(
            collective_id=0, has_side_effects=True, vmem_limit_bytes=56 * 2**20
        ),
        cost_estimate=pl.CostEstimate(flops=13 * 10**9, bytes_accessed=4 * 10**6, transcendentals=400000),
    )(tokens, hidden_grad, gate_weight, up_weight, counts.reshape(N_DOM, 1))
    return mix_gate, mix_up, alpha[:, 0]


def solution(mesh):
    return jax.shard_map(
        local,
        mesh=mesh,
        in_specs=(
            P("dom", "fsdp", None),
            P("dom", None, "fsdp"),
            P("dom", "fsdp"),
            P("dom", "fsdp"),
            P(),
        ),
        out_specs=(P("dom", "fsdp"), P("dom", "fsdp"), P()),
        check_vma=False,
    )
```

```python
import functools

import jax
import jax.numpy as jnp
from jax import lax
from jax.experimental import pallas as pl
from jax.experimental.pallas import tpu as pltpu
from jax.sharding import PartitionSpec as P

STEP_SIZE = 4.0
EPS = 1e-06
MESH = pl.DeviceIdType.MESH

SIDE = 4
N_DOM = 16
N_FSDP = 16
CHUNKS = 4
LANES = 128
ROWS = 256
TOK = 48
TOKENS = 768
D = 4096
PIECES = 4
PIECE = D // PIECES
ORDER = (10, 5, 15, 7, 13, 6, 14, 9, 11, 8, 2, 4, 1, 12, 3)


def wrap(i, n):
    return lax.rem(i + n, n)


def remote(src, dst, ss, rs, **where):
    return pltpu.make_async_remote_copy(
        src_ref=src, dst_ref=dst, send_sem=ss, recv_sem=rs, device_id=where, device_id_type=MESH
    )


def kernel(
    tok_ref, hg_ref, gw_ref, uw_ref, cnt_ref,
    og_ref, ou_ref, oa_ref,
    tokens, tokens_t, weights, grads, stack, acts, mean, scale, part, msg, msg2, ar1, ar2,
    rs_s, rs_r, sb_s, sb_r, w1_s, w1_r, w2_s, w2_r, g_s, g_r, a1_s, a1_r, a2_s, a2_r,
):
    me = lax.axis_index("dom")
    x, y = me // SIDE, lax.rem(me, SIDE)
    f = lax.axis_index("fsdp")
    z, core = f // 2, lax.rem(f, 2)
    way = 1 - 2 * core
    sibling = f + way
    onward = wrap(z + way, 8) * 2 + core

    barrier = pltpu.get_barrier_semaphore()

    @pl.loop(1, N_DOM)
    def _(k):
        pl.semaphore_signal(barrier, inc=1, device_id={"dom": lax.rem(me + k, N_DOM)}, device_id_type=MESH)
        pl.semaphore_signal(barrier, inc=1, device_id={"fsdp": lax.rem(f + k, N_FSDP)}, device_id_type=MESH)

    pl.semaphore_wait(barrier, 2 * (N_DOM - 1))

    def shard(s, c, h):
        owner = wrap(z - s * (1 - 2 * c) + 8, 8) * 2 + c
        return tokens.at[pl.ds(pl.multiple_of(owner * TOK, 16), TOK), pl.ds(h * PIECE, PIECE)]

    def ring(s, h):
        src = tok_ref.at[0, :, pl.ds(h * PIECE, PIECE)] if s == 0 else shard(s, core, h)
        return remote(src, shard(s, core, h), rs_s.at[s, h], rs_r.at[s, h], fsdp=onward)

    def side(s, h):
        src = tok_ref.at[0, :, pl.ds(h * PIECE, PIECE)] if s == 0 else shard(s, core, h)
        return remote(src, shard(s, core, h), sb_s.at[s, h], sb_r.at[s, h], fsdp=sibling)

    def token_step(s):
        for h in range(PIECES):
            here = shard(s, core, h)
            remote(here, here, rs_s.at[s - 1, h], rs_r.at[s - 1, h], fsdp=onward).wait_recv()
            if s < 7:
                ring(s, h).start()
            side(s, h).start()

    def block(kind, c, bx, by, lo=0, n=ROWS):
        return weights.at[kind, c, bx, by, pl.ds(lo, n)]

    def line(kind, c, off, lo=0, n=ROWS):
        if kind == 0:
            return weights.at[kind, c, :, wrap(y + off, SIDE), pl.ds(lo, n)]
        return weights.at[kind, c, wrap(x + off, SIDE), :, pl.ds(lo, n)]

    def near(axis, off):
        if axis == 0:
            return wrap(x + off, SIDE) * SIDE + y
        return x * SIDE + wrap(y + off, SIDE)

    def first(kind, c, off, lo=0, n=ROWS):
        if kind == 0:
            return block(kind, c, wrap(x + off, SIDE), y, lo, n)
        return block(kind, c, x, wrap(y + off, SIDE), lo, n)

    HALF = ROWS // 2

    def w1(kind, c, i):
        axis, to = kind, (1, -1)[i % 2]
        if i < 2:
            src_ref = (gw_ref, uw_ref)[kind]
            src = src_ref.at[:, pl.ds(pl.multiple_of(c * LANES, LANES), LANES)]
            return remote(src, first(kind, c, 0), w1_s.at[kind, c, i], w1_r.at[kind, c, i], dom=near(axis, to))
        part_ = first(kind, c, -to, (i - 2) * HALF, HALF)
        return remote(part_, part_, w1_s.at[kind, c, i], w1_r.at[kind, c, i], dom=near(axis, to))

    def w1_got(kind, c, i):
        to = (1, -1)[i % 2]
        here = first(kind, c, -to) if i < 2 else first(kind, c, 2, (i - 2) * HALF, HALF)
        remote(here, here, w1_s.at[kind, c, i], w1_r.at[kind, c, i], dom=near(kind, to)).wait_recv()

    def w2(kind, c, i):
        axis, to = 1 - kind, (1, -1)[i % 2]
        src = line(kind, c, 0) if i < 2 else line(kind, c, -to, (i - 2) * HALF, HALF)
        return remote(src, src, w2_s.at[kind, c, i], w2_r.at[kind, c, i], dom=near(axis, to))

    def w2_got(kind, c, i):
        to = (1, -1)[i % 2]
        here = line(kind, c, -to) if i < 2 else line(kind, c, 2, (i - 2) * HALF, HALF)
        remote(here, here, w2_s.at[kind, c, i], w2_r.at[kind, c, i], dom=near(1 - kind, to)).wait_recv()

    for h in range(PIECES):
        ring(0, h).start()

    @pl.loop(0, CHUNKS)
    def _(c):
        for kind in range(2):
            for i in range(2):
                w1(kind, c, i).start()

    for h in range(PIECES):
        side(0, h).start()
    tokens[pl.ds(pl.multiple_of(f * TOK, 16), TOK), :] = tok_ref[0]
    for c in range(CHUNKS):
        weights[0, c, x, y] = gw_ref[:, c * LANES : (c + 1) * LANES]
        weights[1, c, x, y] = uw_ref[:, c * LANES : (c + 1) * LANES]

    count = cnt_ref[0]
    for j in range(1, N_DOM):
        count += cnt_ref[j]
    count = jnp.full((1, 2 * LANES), count.astype(jnp.float32))
    for j in range(N_DOM):
        scale[j] = jnp.full((1, 2 * LANES), cnt_ref[j].astype(jnp.float32)) / count
    prior = scale[...].reshape(N_DOM, 2 * LANES)[:, :1]

    def spread_out(column):
        for j in range(N_DOM):
            scale[j] = jnp.broadcast_to(column[j : j + 1, :], (1, 2 * LANES))

    part[...] = jnp.zeros_like(part)

    def stage_a(c):
        for kind in range(2):
            for i in range(2):
                w1_got(kind, c, i)
                w1(kind, c, i + 2).start()

    def stage_b(c):
        for kind in range(2):
            for i in range(2, 4):
                w1_got(kind, c, i)
            for i in range(2):
                w2(kind, c, i).start()

    def stage_c(c):
        for kind in range(2):
            for i in range(2):
                w2_got(kind, c, i)
                w2(kind, c, i + 2).start()

    def stage_d(c):
        for kind in range(2):
            for i in range(2, 4):
                w2_got(kind, c, i)

    token_step(1)
    pl.loop(0, CHUNKS)(stage_a)
    token_step(2)
    pl.loop(0, CHUNKS)(stage_b)
    token_step(3)
    stage_c(0)
    token_step(4)
    stage_c(1)
    token_step(5)
    stage_c(2)
    token_step(6)
    token_step(7)
    stage_c(3)

    @pl.loop(0, 8)
    def _(s):
        for h in range(PIECES):
            here = shard(s, 1 - core, h)
            remote(here, here, sb_s.at[s, h], sb_r.at[s, h], fsdp=sibling).wait_recv()

    @pl.loop(0, D // 256)
    def _(k):
        at = pl.ds(pl.multiple_of(k * 256, 256), 256)
        tokens_t[at, :] = tokens[:, at].T

    def target(k):
        t = ORDER[0]
        for i in range(1, N_DOM - 1):
            t = jnp.where(k == i, ORDER[i], t)
        dx, dy = t // SIDE, lax.rem(t, SIDE)
        dx, dy = dx + core * (dy - dx), dy + core * (dx - dy)
        return wrap(x + dx, SIDE) * SIDE + wrap(y + dy, SIDE)

    def chunk(c):
        stage_d(c)

        @pl.loop(0, TOKENS // 256)
        def _(m):
            at = pl.ds(pl.multiple_of(m * 256, 256), 256)
            w = jnp.concatenate([weights[0, c].reshape(D, LANES), weights[1, c].reshape(D, LANES)], axis=1)
            pre = jnp.dot(tokens[at, :], w, preferred_element_type=jnp.float32)
            gate, up = pre[:, :LANES], pre[:, LANES:]
            g = hg_ref[0, at, pl.ds(pl.multiple_of(c * LANES, LANES), LANES)].astype(jnp.float32)
            s = jax.nn.sigmoid(gate)
            acts[at, :LANES] = (g * up * s * (1.0 + gate * (1.0 - s))).astype(jnp.bfloat16)
            acts[at, LANES:] = (g * gate * s).astype(jnp.bfloat16)

        def block_of(t):
            rows = pl.ds(pl.multiple_of(t * ROWS, ROWS), ROWS)
            out = jnp.dot(tokens_t[rows, :], acts[...], preferred_element_type=jnp.float32)
            return out.astype(jnp.bfloat16)

        @pl.loop(0, N_DOM - 1)
        def _(k):
            t = target(k)
            grads[c, t] = block_of(t)
            remote(grads.at[c, t], stack.at[c, me], g_s.at[c, t], g_r.at[c, me], dom=t).start()

        stack[c, me] = block_of(me)

    pl.loop(0, CHUNKS)(chunk)

    def products(c):
        @pl.loop(1, N_DOM)
        def _(k):
            j = lax.rem(me + k, N_DOM)
            here = stack.at[c, j]
            remote(here, here, g_s.at[c, j], g_r.at[c, j], dom=j).wait_recv()

        @pl.loop(0, ROWS // 32)
        def _(r):
            at = pl.ds(pl.multiple_of(r * 32, 32), 32)
            total = scale[0] * stack[c, 0, at, :].astype(jnp.float32)
            for j in range(1, N_DOM):
                total += scale[j] * stack[c, j, at, :].astype(jnp.float32)
            mean[at, :] = total

        @pl.loop(0, N_DOM)
        def _(j):
            toward = jnp.zeros((8, 2 * LANES), jnp.float32)
            own = jnp.zeros((8, 2 * LANES), jnp.float32)
            for r in range(ROWS // 32):
                at = pl.ds(r * 32, 32)
                g = stack[c, j, at, :].astype(jnp.float32)
                toward += jnp.sum((g * mean[at, :]).reshape(4, 8, 2 * LANES), axis=0)
                own += jnp.sum((g * g).reshape(4, 8, 2 * LANES), axis=0)
            toward = jnp.sum(toward, axis=0, keepdims=True)
            own = jnp.sum(own, axis=0, keepdims=True)
            part[j] += toward[:, :LANES] + toward[:, LANES:]
            part[N_DOM + j] += own[:, :LANES] + own[:, LANES:]

    pl.loop(0, CHUNKS)(products)

    group = lax.broadcasted_iota(jnp.int32, (8, LANES), 1) // 32
    packed = jnp.zeros((8, LANES), jnp.float32)
    sums = part[...].reshape(2 * N_DOM, LANES)
    for q in range(4):
        own = sums[8 * q : 8 * q + 8]
        own = own + pltpu.roll(own, 64, 1)
        own = own + pltpu.roll(own, 32, 1)
        packed = jnp.where(group == q, own, packed)
    msg[...] = packed
    ar1[me] = packed

    @pl.loop(1, N_DOM)
    def _(k):
        t = lax.rem(me + k, N_DOM)
        remote(msg, ar1.at[me], a1_s.at[t], a1_r.at[me], dom=t).start()

    @pl.loop(1, N_DOM)
    def _(k):
        t = lax.rem(me + k, N_DOM)
        remote(msg, ar1.at[t], a1_s.at[t], a1_r.at[t], dom=t).wait_recv()

    total = ar1[0]
    for j in range(1, N_DOM):
        total += ar1[j]
    msg2[...] = total
    ar2[f] = total

    @pl.loop(1, N_FSDP)
    def _(k):
        t = lax.rem(f + k, N_FSDP)
        remote(msg2, ar2.at[f], a2_s.at[t], a2_r.at[f], fsdp=t).start()

    @pl.loop(1, N_FSDP)
    def _(k):
        t = lax.rem(f + k, N_FSDP)
        remote(msg2, ar2.at[t], a2_s.at[t], a2_r.at[t], fsdp=t).wait_recv()

    total = ar2[0]
    for j in range(1, N_FSDP):
        total += ar2[j]
    total = [jnp.sum(jnp.where(group == q, total, 0.0), axis=1, keepdims=True) for q in range(4)]
    toward, own = jnp.concatenate(total[:2], axis=0), jnp.concatenate(total[2:], axis=0)
    spread = jnp.sum(prior * toward, axis=0, keepdims=True)
    cosine = toward / jnp.sqrt((own + EPS) * (spread + EPS))
    scaled = prior * jnp.exp(STEP_SIZE * cosine)
    alpha = scaled / jnp.sum(scaled, axis=0, keepdims=True)
    row = lax.broadcasted_iota(jnp.int32, (N_DOM, N_DOM), 0)
    lane = lax.broadcasted_iota(jnp.int32, (N_DOM, N_DOM), 1)
    oa_ref[...] = jnp.sum(jnp.where(row == lane, alpha, 0.0), axis=0, keepdims=True)
    spread_out(alpha)

    for c in range(CHUNKS):
        cols = pl.ds(c * LANES, LANES)

        @pl.loop(0, ROWS // 32)
        def _(r):
            at = pl.ds(pl.multiple_of(r * 32, 32), 32)
            mix = scale[0] * stack[c, 0, at, :].astype(jnp.float32)
            for j in range(1, N_DOM):
                mix += scale[j] * stack[c, j, at, :].astype(jnp.float32)
            og_ref[at, cols] = mix[:, :LANES]
            ou_ref[at, cols] = mix[:, LANES:]

    for h in range(PIECES):
        for s in range(7):
            ring(s, h).wait_send()
        for s in range(8):
            side(s, h).wait_send()

    @pl.loop(0, CHUNKS)
    def _(c):
        for kind in range(2):
            for i in range(4):
                w1(kind, c, i).wait_send()
                w2(kind, c, i).wait_send()

        @pl.loop(1, N_DOM)
        def _(k):
            t = lax.rem(me + k, N_DOM)
            remote(grads.at[c, t], stack.at[c, me], g_s.at[c, t], g_r.at[c, me], dom=t).wait_send()

    @pl.loop(1, N_DOM)
    def _(k):
        t = lax.rem(me + k, N_DOM)
        remote(msg, ar1.at[me], a1_s.at[t], a1_r.at[me], dom=t).wait_send()
        t = lax.rem(f + k, N_FSDP)
        remote(msg2, ar2.at[f], a2_s.at[t], a2_r.at[f], fsdp=t).wait_send()


def local(tokens, hidden_grad, gate_weight, up_weight, counts):
    vmem = pl.BlockSpec(memory_space=pltpu.VMEM)
    dma = pltpu.SemaphoreType.DMA
    bf16, f32 = jnp.bfloat16, jnp.float32
    mix_gate, mix_up, alpha = pl.pallas_call(
        kernel,
        out_shape=(
            jax.ShapeDtypeStruct((ROWS, CHUNKS * LANES), f32),
            jax.ShapeDtypeStruct((ROWS, CHUNKS * LANES), f32),
            jax.ShapeDtypeStruct((1, N_DOM), f32),
        ),
        in_specs=[vmem] * 4 + [pl.BlockSpec(memory_space=pltpu.SMEM)],
        out_specs=(vmem,) * 3,
        scratch_shapes=[
            pltpu.VMEM((TOKENS, D), bf16),
            pltpu.VMEM((D, TOKENS), bf16),
            pltpu.VMEM((2, CHUNKS, SIDE, SIDE, ROWS, LANES), bf16),
            pltpu.VMEM((CHUNKS, N_DOM, ROWS, 2 * LANES), bf16),
            pltpu.VMEM((CHUNKS, N_DOM, ROWS, 2 * LANES), bf16),
            pltpu.VMEM((TOKENS, 2 * LANES), bf16),
            pltpu.VMEM((ROWS, 2 * LANES), f32),
            pltpu.VMEM((N_DOM, 1, 2 * LANES), f32),
            pltpu.VMEM((2 * N_DOM, 1, LANES), f32),
            pltpu.VMEM((8, LANES), f32),
            pltpu.VMEM((8, LANES), f32),
            pltpu.VMEM((N_DOM, 8, LANES), f32),
            pltpu.VMEM((N_FSDP, 8, LANES), f32),
            dma((7, PIECES)), dma((7, PIECES)), dma((8, PIECES)), dma((8, PIECES)),
            dma((2, CHUNKS, 4)), dma((2, CHUNKS, 4)), dma((2, CHUNKS, 4)), dma((2, CHUNKS, 4)),
            dma((CHUNKS, N_DOM)), dma((CHUNKS, N_DOM)),
            dma((N_DOM,)), dma((N_DOM,)), dma((N_FSDP,)), dma((N_FSDP,)),
        ],
        compiler_params=pltpu.CompilerParams(
            collective_id=0, has_side_effects=True, vmem_limit_bytes=56 * 2**20
        ),
        cost_estimate=pl.CostEstimate(flops=13 * 10**9, bytes_accessed=4 * 10**6, transcendentals=400000),
    )(tokens, hidden_grad, gate_weight, up_weight, counts)
    return mix_gate, mix_up, alpha.reshape(N_DOM)


def solution(mesh):
    return jax.shard_map(
        local,
        mesh=mesh,
        in_specs=(
            P("dom", "fsdp", None),
            P("dom", None, "fsdp"),
            P("dom", "fsdp"),
            P("dom", "fsdp"),
            P(),
        ),
        out_specs=(P("dom", "fsdp"), P("dom", "fsdp"), P()),
        check_vma=False,
    )
```

```python
import functools

import jax
import jax.numpy as jnp
from jax import lax
from jax.experimental import pallas as pl
from jax.experimental.pallas import tpu as pltpu
from jax.sharding import PartitionSpec as P

STEP_SIZE = 4.0
EPS = 1e-06
MESH = pl.DeviceIdType.MESH

SIDE = 4
N_DOM = 16
N_FSDP = 16
CHUNKS = 4
LANES = 128
ROWS = 256
TOK = 48
TOKENS = 768
D = 4096
PIECES = 2
PIECE = D // PIECES
ORDER = (10, 5, 15, 7, 13, 6, 14, 9, 11, 8, 2, 4, 1, 12, 3)


def wrap(i, n):
    return lax.rem(i + n, n)


def remote(src, dst, ss, rs, **where):
    return pltpu.make_async_remote_copy(
        src_ref=src, dst_ref=dst, send_sem=ss, recv_sem=rs, device_id=where, device_id_type=MESH
    )


def kernel(
    tok_ref, hg_ref, gw_ref, uw_ref, cnt_ref,
    og_ref, ou_ref, oa_ref,
    tokens, tokens_t, weights, grads, stack, acts, mean, scale, part, msg, msg2, ar1, ar2,
    rs_s, rs_r, sb_s, sb_r, w1_s, w1_r, w2_s, w2_r, g_s, g_r, a1_s, a1_r, a2_s, a2_r,
):
    me = lax.axis_index("dom")
    x, y = me // SIDE, lax.rem(me, SIDE)
    f = lax.axis_index("fsdp")
    z, core = f // 2, lax.rem(f, 2)
    way = 1 - 2 * core
    sibling = f + way
    onward = wrap(z + way, 8) * 2 + core
    behind = wrap(z - way, 8) * 2 + core

    barrier = pltpu.get_barrier_semaphore()

    for where in (
        {"dom": wrap(x + 1, SIDE) * SIDE + y},
        {"dom": wrap(x - 1, SIDE) * SIDE + y},
        {"dom": x * SIDE + wrap(y + 1, SIDE)},
        {"dom": x * SIDE + wrap(y - 1, SIDE)},
        {"fsdp": onward},
        {"fsdp": behind},
        {"fsdp": sibling},
    ):
        pl.semaphore_signal(barrier, inc=1, device_id=where, device_id_type=MESH)
    pl.semaphore_wait(barrier, 7)

    def shard(s, c, h):
        owner = wrap(z - s * (1 - 2 * c) + 8, 8) * 2 + c
        return tokens.at[pl.ds(pl.multiple_of(owner * TOK, 16), TOK), pl.ds(h * PIECE, PIECE)]

    def ring(s, h, back=0):
        src = tok_ref.at[0, :, pl.ds(h * PIECE, PIECE)] if s == 0 else shard(s, core, h)
        to = (onward, behind)[back]
        i = 4 - s if back else s
        return remote(src, shard(s, core, h), rs_s.at[i, h], rs_r.at[i, h], fsdp=to)

    def side(s, h):
        src = tok_ref.at[0, :, pl.ds(h * PIECE, PIECE)] if s == 0 else shard(s, core, h)
        return remote(src, shard(s, core, h), sb_s.at[s + 3, h], sb_r.at[s + 3, h], fsdp=sibling)

    def token_step(s):
        for h in range(PIECES):
            here = shard(s, core, h)
            i = s - 1 if s > 0 else 3 - s
            remote(here, here, rs_s.at[i, h], rs_r.at[i, h], fsdp=onward).wait_recv()
            if 0 < s < 4:
                ring(s, h).start()
            if -3 < s < 0:
                ring(s, h, 1).start()
            side(s, h).start()

    def block(kind, c, bx, by, lo=0, n=ROWS):
        return weights.at[kind, c, bx, by, pl.ds(lo, n)]

    def line(kind, c, off, lo=0, n=ROWS):
        if kind == 0:
            return weights.at[kind, c, :, wrap(y + off, SIDE), pl.ds(lo, n)]
        return weights.at[kind, c, wrap(x + off, SIDE), :, pl.ds(lo, n)]

    def near(axis, off):
        if axis == 0:
            return wrap(x + off, SIDE) * SIDE + y
        return x * SIDE + wrap(y + off, SIDE)

    def first(kind, c, off, lo=0, n=ROWS):
        if kind == 0:
            return block(kind, c, wrap(x + off, SIDE), y, lo, n)
        return block(kind, c, x, wrap(y + off, SIDE), lo, n)

    HALF = ROWS // 2

    def w1(kind, c, i):
        axis, to = kind, (1, -1)[i % 2]
        if i < 2:
            src_ref = (gw_ref, uw_ref)[kind]
            src = src_ref.at[:, pl.ds(pl.multiple_of(c * LANES, LANES), LANES)]
            return remote(src, first(kind, c, 0), w1_s.at[kind, c, i], w1_r.at[kind, c, i], dom=near(axis, to))
        part_ = first(kind, c, -to, (i - 2) * HALF, HALF)
        return remote(part_, part_, w1_s.at[kind, c, i], w1_r.at[kind, c, i], dom=near(axis, to))

    def w1_got(kind, c, i):
        to = (1, -1)[i % 2]
        here = first(kind, c, -to) if i < 2 else first(kind, c, 2, (i - 2) * HALF, HALF)
        remote(here, here, w1_s.at[kind, c, i], w1_r.at[kind, c, i], dom=near(kind, to)).wait_recv()

    def w2(kind, c, i):
        axis, to = 1 - kind, (1, -1)[i % 2]
        src = line(kind, c, 0) if i < 2 else line(kind, c, -to, (i - 2) * HALF, HALF)
        return remote(src, src, w2_s.at[kind, c, i], w2_r.at[kind, c, i], dom=near(axis, to))

    def w2_got(kind, c, i):
        to = (1, -1)[i % 2]
        here = line(kind, c, -to) if i < 2 else line(kind, c, 2, (i - 2) * HALF, HALF)
        remote(here, here, w2_s.at[kind, c, i], w2_r.at[kind, c, i], dom=near(1 - kind, to)).wait_recv()

    for h in range(PIECES):
        ring(0, h).start()
        ring(0, h, 1).start()

    @pl.loop(0, CHUNKS)
    def _(c):
        for kind in range(2):
            for i in range(2):
                w1(kind, c, i).start()

    for h in range(PIECES):
        side(0, h).start()
    tokens[pl.ds(pl.multiple_of(f * TOK, 16), TOK), :] = tok_ref[0]
    for c in range(CHUNKS):
        weights[0, c, x, y] = gw_ref[:, c * LANES : (c + 1) * LANES]
        weights[1, c, x, y] = uw_ref[:, c * LANES : (c + 1) * LANES]

    count = cnt_ref[0]
    for j in range(1, N_DOM):
        count += cnt_ref[j]
    count = jnp.full((1, 2 * LANES), count.astype(jnp.float32))
    for j in range(N_DOM):
        scale[j] = jnp.full((1, 2 * LANES), cnt_ref[j].astype(jnp.float32)) / count
    prior = scale[...].reshape(N_DOM, 2 * LANES)[:, :1]

    def spread_out(column):
        for j in range(N_DOM):
            scale[j] = jnp.broadcast_to(column[j : j + 1, :], (1, 2 * LANES))

    part[...] = jnp.zeros_like(part)

    def stage_a(c):
        for kind in range(2):
            for i in range(2):
                w1_got(kind, c, i)
                w1(kind, c, i + 2).start()

    def stage_b(c):
        for kind in range(2):
            for i in range(2, 4):
                w1_got(kind, c, i)
            for i in range(2):
                w2(kind, c, i).start()

    def stage_c(c):
        for kind in range(2):
            for i in range(2):
                w2_got(kind, c, i)
                w2(kind, c, i + 2).start()

    def stage_d(c):
        for kind in range(2):
            for i in range(2, 4):
                w2_got(kind, c, i)

    pl.loop(0, CHUNKS)(stage_a)
    token_step(1)
    token_step(-1)
    stage_b(0)
    stage_b(1)
    stage_b(2)
    stage_b(3)
    token_step(2)
    token_step(-2)
    stage_c(0)
    stage_c(1)
    token_step(3)
    token_step(-3)
    token_step(4)
    stage_c(2)

    @pl.loop(0, 8)
    def _(s):
        for h in range(PIECES):
            here = shard(s - 3, 1 - core, h)
            remote(here, here, sb_s.at[s, h], sb_r.at[s, h], fsdp=sibling).wait_recv()

    def target(k):
        t = ORDER[0]
        for i in range(1, N_DOM - 1):
            t = jnp.where(k == i, ORDER[i], t)
        dx, dy = t // SIDE, lax.rem(t, SIDE)
        dx, dy = dx + core * (dy - dx), dy + core * (dx - dy)
        return wrap(x + dx, SIDE) * SIDE + wrap(y + dy, SIDE)

    def activations(c):
        stage_d(c)

        @pl.loop(0, TOKENS // 256)
        def _(m):
            at = pl.ds(pl.multiple_of(m * 256, 256), 256)
            w = jnp.concatenate([weights[0, c].reshape(D, LANES), weights[1, c].reshape(D, LANES)], axis=1)
            pre = jnp.dot(tokens[at, :], w, preferred_element_type=jnp.float32)
            gate, up = pre[:, :LANES], pre[:, LANES:]
            g = hg_ref[0, at, pl.ds(pl.multiple_of(c * LANES, LANES), LANES)].astype(jnp.float32)
            s = jax.nn.sigmoid(gate)
            acts[at, :LANES] = (g * up * s * (1.0 + gate * (1.0 - s))).astype(jnp.bfloat16)
            acts[at, LANES:] = (g * gate * s).astype(jnp.bfloat16)

    def gradients(c, turn=False):
        def block_of(t):
            rows = pl.ds(pl.multiple_of(t * ROWS, ROWS), ROWS)
            if turn:
                tokens_t[rows, :] = tokens[:, rows].T
            out = jnp.dot(tokens_t[rows, :], acts[...], preferred_element_type=jnp.float32)
            return out.astype(jnp.bfloat16)

        @pl.loop(0, N_DOM - 1)
        def _(k):
            t = target(k)
            grads[c, t] = block_of(t)
            remote(grads.at[c, t], stack.at[c, me], g_s.at[c, t], g_r.at[c, me], dom=t).start()

        stack[c, me] = block_of(me)

    def chunk(c):
        activations(c)
        gradients(c)

    activations(0)
    gradients(0, True)
    stage_c(3)
    pl.loop(1, CHUNKS)(chunk)

    for h in range(PIECES):
        for s in range(4):
            ring(s, h).wait_send()
        for s in range(3):
            ring(-s, h, 1).wait_send()
        for s in range(-3, 5):
            side(s, h).wait_send()

    @pl.loop(0, CHUNKS)
    def _(c):
        for kind in range(2):
            for i in range(4):
                w1(kind, c, i).wait_send()
                w2(kind, c, i).wait_send()

    def products(c):
        @pl.loop(1, N_DOM)
        def _(k):
            j = lax.rem(me + k, N_DOM)
            here = stack.at[c, j]
            remote(grads.at[c, j], here, g_s.at[c, j], g_r.at[c, j], dom=j).wait_send()
            remote(here, here, g_s.at[c, j], g_r.at[c, j], dom=j).wait_recv()

        @pl.loop(0, ROWS // 32)
        def _(r):
            at = pl.ds(pl.multiple_of(r * 32, 32), 32)
            total = scale[0] * stack[c, 0, at, :].astype(jnp.float32)
            for j in range(1, N_DOM):
                total += scale[j] * stack[c, j, at, :].astype(jnp.float32)
            mean[at, :] = total

        @pl.loop(0, N_DOM)
        def _(j):
            toward = jnp.zeros((8, 2 * LANES), jnp.float32)
            own = jnp.zeros((8, 2 * LANES), jnp.float32)
            for r in range(ROWS // 32):
                at = pl.ds(r * 32, 32)
                g = stack[c, j, at, :].astype(jnp.float32)
                toward += jnp.sum((g * mean[at, :]).reshape(4, 8, 2 * LANES), axis=0)
                own += jnp.sum((g * g).reshape(4, 8, 2 * LANES), axis=0)
            toward = jnp.sum(toward, axis=0, keepdims=True)
            own = jnp.sum(own, axis=0, keepdims=True)
            part[j] += toward[:, :LANES] + toward[:, LANES:]
            part[N_DOM + j] += own[:, :LANES] + own[:, LANES:]

    pl.loop(0, CHUNKS)(products)

    group = lax.broadcasted_iota(jnp.int32, (8, LANES), 1) // 32
    packed = jnp.zeros((8, LANES), jnp.float32)
    sums = part[...].reshape(2 * N_DOM, LANES)
    for q in range(4):
        own = sums[8 * q : 8 * q + 8]
        own = own + pltpu.roll(own, 64, 1)
        own = own + pltpu.roll(own, 32, 1)
        packed = jnp.where(group == q, own, packed)
    msg[...] = packed
    ar1[me] = packed

    @pl.loop(1, N_DOM)
    def _(k):
        t = lax.rem(me + k, N_DOM)
        remote(msg, ar1.at[me], a1_s.at[t], a1_r.at[me], dom=t).start()

    @pl.loop(1, N_DOM)
    def _(k):
        t = lax.rem(me + k, N_DOM)
        remote(msg, ar1.at[t], a1_s.at[t], a1_r.at[t], dom=t).wait_recv()

    total = ar1[0]
    for j in range(1, N_DOM):
        total += ar1[j]
    msg2[...] = total
    ar2[f] = total

    @pl.loop(1, N_FSDP)
    def _(k):
        t = lax.rem(f + k, N_FSDP)
        remote(msg2, ar2.at[f], a2_s.at[t], a2_r.at[f], fsdp=t).start()

    @pl.loop(1, N_FSDP)
    def _(k):
        t = lax.rem(f + k, N_FSDP)
        remote(msg2, ar2.at[t], a2_s.at[t], a2_r.at[t], fsdp=t).wait_recv()

    total = ar2[0]
    for j in range(1, N_FSDP):
        total += ar2[j]
    for k in range(1, N_DOM):
        t = lax.rem(me + k, N_DOM)
        remote(msg, ar1.at[me], a1_s.at[t], a1_r.at[me], dom=t).wait_send()
        t = lax.rem(f + k, N_FSDP)
        remote(msg2, ar2.at[f], a2_s.at[t], a2_r.at[f], fsdp=t).wait_send()

    total = [jnp.sum(jnp.where(group == q, total, 0.0), axis=1, keepdims=True) for q in range(4)]
    toward, own = jnp.concatenate(total[:2], axis=0), jnp.concatenate(total[2:], axis=0)
    spread = jnp.sum(prior * toward, axis=0, keepdims=True)
    cosine = toward / jnp.sqrt((own + EPS) * (spread + EPS))
    scaled = prior * jnp.exp(STEP_SIZE * cosine)
    alpha = scaled / jnp.sum(scaled, axis=0, keepdims=True)
    row = lax.broadcasted_iota(jnp.int32, (N_DOM, N_DOM), 0)
    lane = lax.broadcasted_iota(jnp.int32, (N_DOM, N_DOM), 1)
    oa_ref[...] = jnp.sum(jnp.where(row == lane, alpha, 0.0), axis=0, keepdims=True)
    spread_out(alpha)

    for c in range(CHUNKS):
        cols = pl.ds(c * LANES, LANES)

        @pl.loop(0, ROWS // 32)
        def _(r):
            at = pl.ds(pl.multiple_of(r * 32, 32), 32)
            mix = scale[0] * stack[c, 0, at, :].astype(jnp.float32)
            for j in range(1, N_DOM):
                mix += scale[j] * stack[c, j, at, :].astype(jnp.float32)
            og_ref[at, cols] = mix[:, :LANES]
            ou_ref[at, cols] = mix[:, LANES:]


def local(tokens, hidden_grad, gate_weight, up_weight, counts):
    vmem = pl.BlockSpec(memory_space=pltpu.VMEM)
    dma = pltpu.SemaphoreType.DMA
    bf16, f32 = jnp.bfloat16, jnp.float32
    mix_gate, mix_up, alpha = pl.pallas_call(
        kernel,
        out_shape=(
            jax.ShapeDtypeStruct((ROWS, CHUNKS * LANES), f32),
            jax.ShapeDtypeStruct((ROWS, CHUNKS * LANES), f32),
            jax.ShapeDtypeStruct((1, N_DOM), f32),
        ),
        in_specs=[vmem] * 4 + [pl.BlockSpec(memory_space=pltpu.SMEM)],
        out_specs=(vmem,) * 3,
        scratch_shapes=[
            pltpu.VMEM((TOKENS, D), bf16),
            pltpu.VMEM((D, TOKENS), bf16),
            pltpu.VMEM((2, CHUNKS, SIDE, SIDE, ROWS, LANES), bf16),
            pltpu.VMEM((CHUNKS, N_DOM, ROWS, 2 * LANES), bf16),
            pltpu.VMEM((CHUNKS, N_DOM, ROWS, 2 * LANES), bf16),
            pltpu.VMEM((TOKENS, 2 * LANES), bf16),
            pltpu.VMEM((ROWS, 2 * LANES), f32),
            pltpu.VMEM((N_DOM, 1, 2 * LANES), f32),
            pltpu.VMEM((2 * N_DOM, 1, LANES), f32),
            pltpu.VMEM((8, LANES), f32),
            pltpu.VMEM((8, LANES), f32),
            pltpu.VMEM((N_DOM, 8, LANES), f32),
            pltpu.VMEM((N_FSDP, 8, LANES), f32),
            dma((7, PIECES)), dma((7, PIECES)), dma((8, PIECES)), dma((8, PIECES)),
            dma((2, CHUNKS, 4)), dma((2, CHUNKS, 4)), dma((2, CHUNKS, 4)), dma((2, CHUNKS, 4)),
            dma((CHUNKS, N_DOM)), dma((CHUNKS, N_DOM)),
            dma((N_DOM,)), dma((N_DOM,)), dma((N_FSDP,)), dma((N_FSDP,)),
        ],
        compiler_params=pltpu.CompilerParams(
            collective_id=0, has_side_effects=True, vmem_limit_bytes=56 * 2**20
        ),
        cost_estimate=pl.CostEstimate(flops=13 * 10**9, bytes_accessed=4 * 10**6, transcendentals=400000),
    )(tokens, hidden_grad, gate_weight, up_weight, counts)
    return mix_gate, mix_up, alpha.reshape(N_DOM)


def solution(mesh):
    return jax.shard_map(
        local,
        mesh=mesh,
        in_specs=(
            P("dom", "fsdp", None),
            P("dom", None, "fsdp"),
            P("dom", "fsdp"),
            P("dom", "fsdp"),
            P(),
        ),
        out_specs=(P("dom", "fsdp"), P("dom", "fsdp"), P()),
        check_vma=False,
    )
```

```python
import functools

import jax
import jax.numpy as jnp
from jax import lax
from jax.experimental import pallas as pl
from jax.experimental.pallas import tpu as pltpu
from jax.sharding import PartitionSpec as P

STEP_SIZE = 4.0
EPS = 1e-06
MESH = pl.DeviceIdType.MESH

SIDE = 4
N_DOM = 16
N_FSDP = 16
SHARED = 2
CHUNKS = 2
LANES = 128
ROWS = 256
TOK = 48
TOKENS = 768
D = 4096
PIECES = 2
PIECE = D // PIECES
ORDER = (5, 3, 7, 4, 2, 6, 1)


def wrap(i, n):
    return lax.rem(i + n, n)


def remote(src, dst, ss, rs, **where):
    return pltpu.make_async_remote_copy(
        src_ref=src, dst_ref=dst, send_sem=ss, recv_sem=rs, device_id=where, device_id_type=MESH
    )


def kernel(
    tok_ref, hg_ref, gw_ref, uw_ref, cnt_ref,
    og_ref, ou_ref, oa_ref,
    hg, tokens, tokens_t, weights, grads, stack, acts, mean, scale, part, msg, msg2, ar1, ar2, mix_s, mix_r,
    rs_s, rs_r, sb_s, sb_r, sw_s, sw_r, h_s, h_r, w1_s, w1_r, w2_s, w2_r, g_s, g_r, a1_s, a1_r, a2_s, a2_r, m_s, m_r,
):
    me = lax.axis_index("dom")
    x, y = me // SIDE, lax.rem(me, SIDE)
    f = lax.axis_index("fsdp")
    z, core = f // 2, lax.rem(f, 2)
    way = 1 - 2 * core
    sibling = f + way
    onward = wrap(z + way, 8) * 2 + core
    behind = wrap(z - way, 8) * 2 + core
    anti = wrap(x + 2, SIDE) * SIDE + wrap(y + 2, SIDE)
    u, v = x + core * (y - x), y + core * (x - y)

    def at_uv(u_, v_):
        return u_ * (4 - 3 * core) + v_ * (1 + 3 * core)

    def near_u(off):
        return at_uv(wrap(u + off, SIDE), v)

    def near_v(off):
        return at_uv(u, wrap(v + off, SIDE))

    def toward_pair(c):
        return 1 - 2 * lax.rem(v + c, 2)

    def half(c, v_):
        return lax.rem((v_ + c) // 2, 2)

    def columns(c, h):
        return pl.ds(pl.multiple_of((2 * c + h) * LANES, LANES), LANES)

    barrier = pltpu.get_barrier_semaphore()
    for where in (
        {"dom": near_u(1)},
        {"dom": near_u(-1)},
        {"dom": near_v(1)},
        {"dom": near_v(-1)},
        {"dom": near_v(2)},
        {"dom": anti},
        {"fsdp": onward},
        {"fsdp": behind},
        {"fsdp": sibling},
    ):
        pl.semaphore_signal(barrier, inc=1, device_id=where, device_id_type=MESH)
    pl.semaphore_wait(barrier, 9)

    def shard(w, s, c, h):
        owner = wrap(z - s * (1 - 2 * c) + 8, 8) * 2 + c
        return tokens.at[w, pl.ds(pl.multiple_of(owner * TOK, 16), TOK), pl.ds(h * PIECE, PIECE)]

    def source(w, s, h):
        if w == 0 and s == 0:
            return tok_ref.at[0, :, pl.ds(h * PIECE, PIECE)]
        return shard(w, s, core, h)

    def ring(w, s, h, back=0):
        i = 4 - s if back else s
        return remote(
            source(w, s, h), shard(w, s, core, h), rs_s.at[w, i, h], rs_r.at[w, i, h], fsdp=(onward, behind)[back]
        )

    def side(w, s, h):
        return remote(source(w, s, h), shard(w, s, core, h), sb_s.at[w, s + 3, h], sb_r.at[w, s + 3, h], fsdp=sibling)

    def token_start(w):
        for h in range(PIECES):
            ring(w, 0, h).start()
            ring(w, 0, h, 1).start()

    def token_step(w, s):
        for h in range(PIECES):
            here = shard(w, s, core, h)
            i = s - 1 if s > 0 else 3 - s
            remote(here, here, rs_s.at[w, i, h], rs_r.at[w, i, h], fsdp=onward).wait_recv()
            if 0 < s < 4:
                ring(w, s, h).start()
            if -3 < s < 0:
                ring(w, s, h, 1).start()
            side(w, s, h).start()

    def token_side(w):
        @pl.loop(0, 8)
        def _(s):
            for h in range(PIECES):
                here = shard(w, s - 3, 1 - core, h)
                remote(here, here, sb_s.at[w, s, h], sb_r.at[w, s, h], fsdp=sibling).wait_recv()

    own_rows = pl.ds(pl.multiple_of(f * TOK, 16), TOK)

    def swap():
        return remote(tok_ref.at[0], tokens.at[1, own_rows], sw_s.at[0], sw_r.at[0], dom=anti)

    def swap_hg(c):
        return remote(hg_ref.at[0, :, columns(c, 1 - half(c, v))], hg.at[1, c], h_s.at[c], h_r.at[c], dom=anti)

    def w1(c, kind, o):
        to = wrap(v + o, SIDE)
        src = (gw_ref, uw_ref)[kind].at[:, columns(c, half(c, to))]
        return remote(src, weights.at[c, kind, x, y], w1_s.at[c, kind, o], w1_r.at[c, kind, o], dom=at_uv(u, to))

    def w1_got(c, kind, o):
        d = near_v(-o)
        here = weights.at[c, kind, d // SIDE, lax.rem(d, SIDE)]
        remote(here, here, w1_s.at[c, kind, o], w1_r.at[c, kind, o], dom=d).wait_recv()

    MID = ROWS // 2

    def line(axis, c, off, lo=0, n=ROWS):
        at = wrap(u + off, SIDE)
        if axis == 0:
            return weights.at[c, :, at, :, pl.ds(lo, n)]
        return weights.at[c, :, :, at, pl.ds(lo, n)]

    def w2(axis, c, i):
        to = (1, -1)[i % 2]
        src = line(axis, c, 0) if i < 2 else line(axis, c, -to, (i - 2) * MID, MID)
        return remote(src, src, w2_s.at[c, i], w2_r.at[c, i], dom=near_u(to))

    def w2_got(axis, c, i):
        to = (1, -1)[i % 2]
        here = line(axis, c, -to) if i < 2 else line(axis, c, 2, (i - 2) * MID, MID)
        remote(here, here, w2_s.at[c, i], w2_r.at[c, i], dom=near_u(to)).wait_recv()

    def by_core(do):
        for axis in range(2):
            pl.when(core == axis)(functools.partial(do, axis))

    def stage_b(axis):
        for c in range(CHUNKS):
            for i in range(2):
                w2(axis, c, i).start()

    def stage_c(c, axis):
        for i in range(2):
            w2_got(axis, c, i)
            w2(axis, c, i + 2).start()

    def stage_d(c, axis):
        for i in range(2, 4):
            w2_got(axis, c, i)

    token_start(0)
    swap().start()
    for c in range(CHUNKS):
        for kind in range(2):
            for o in (2, 1, 3):
                w1(c, kind, o).start()
    for h in range(PIECES):
        side(0, 0, h).start()

    tokens[0, own_rows, :] = tok_ref[0]
    for c in range(CHUNKS):
        cols = columns(c, half(c, v))
        weights[c, 0, x, y] = gw_ref[:, cols]
        weights[c, 1, x, y] = uw_ref[:, cols]
        hg[0, c] = hg_ref[0, :, cols]

    def spread_out(column):
        for j in range(N_DOM):
            scale[j] = jnp.broadcast_to(column[j : j + 1, :], (1, 2 * LANES))

    count = cnt_ref[0]
    for j in range(1, N_DOM):
        count += cnt_ref[j]
    count = jnp.full((1, 2 * LANES), count.astype(jnp.float32))
    for j in range(N_DOM):
        scale[j] = jnp.full((1, 2 * LANES), cnt_ref[j].astype(jnp.float32)) / count
    prior = scale[...].reshape(N_DOM, 2 * LANES)[:, :1]
    part[...] = jnp.zeros_like(part)

    for c in range(CHUNKS):
        for kind in range(2):
            for o in (2, 1, 3):
                w1_got(c, kind, o)
    by_core(stage_b)
    for c in range(CHUNKS):
        swap_hg(c).start()
    token_step(0, 1)
    token_step(0, -1)
    by_core(functools.partial(stage_c, 0))
    token_step(0, 2)
    token_step(0, -2)
    by_core(functools.partial(stage_c, 1))
    remote(tokens.at[1, own_rows], tokens.at[1, own_rows], sw_s.at[0], sw_r.at[0], dom=anti).wait_recv()
    token_step(0, 3)
    token_step(0, -3)
    token_start(1)
    for h in range(PIECES):
        side(1, 0, h).start()
    token_step(0, 4)
    token_side(0)
    by_core(functools.partial(stage_d, 0))

    def activations(w, c):
        @pl.loop(0, TOKENS // 256)
        def _(m):
            at = pl.ds(pl.multiple_of(m * 256, 256), 256)
            wide = jnp.concatenate([weights[c, 0].reshape(D, LANES), weights[c, 1].reshape(D, LANES)], axis=1)
            pre = jnp.dot(tokens[w, at, :], wide, preferred_element_type=jnp.float32)
            gate, up = pre[:, :LANES], pre[:, LANES:]
            g = hg[w, c, at, :].astype(jnp.float32)
            s = jax.nn.sigmoid(gate)
            acts[at, :LANES] = (g * up * s * (1.0 + gate * (1.0 - s))).astype(jnp.bfloat16)
            acts[at, LANES:] = (g * gate * s).astype(jnp.bfloat16)

    def gradients(w, c, turn):
        way_v = toward_pair(c)
        domain = (me, anti)[w]

        def block_of(d):
            rows = pl.ds(pl.multiple_of(d * ROWS, ROWS), ROWS)
            if turn:
                tokens_t[w, rows, :] = tokens[w, :, rows].T
            out = jnp.dot(tokens_t[w, rows, :], acts[...], preferred_element_type=jnp.float32)
            return out.astype(jnp.bfloat16)

        @pl.loop(0, 7)
        def _(k):
            i = ORDER[0]
            for n in range(1, 7):
                i = jnp.where(k == n, ORDER[n], i)
            du, pair = i // 2, lax.rem(i, 2)
            u_ = wrap(u + du, SIDE)
            first = wrap(v + pair * way_v, SIDE)
            grads[w, c, i, :ROWS, :] = block_of(at_uv(u_, first))
            grads[w, c, i, ROWS:, :] = block_of(at_uv(u_, wrap(v - way_v + 3 * pair * way_v + 4, SIDE)))
            remote(
                grads.at[w, c, i], stack.at[c, domain], g_s.at[w, c, i], g_r.at[w, c, i], dom=at_uv(u_, first)
            ).start()

        stack[c, domain, :ROWS, :] = block_of(me)
        stack[c, domain, ROWS:, :] = block_of(near_v(-way_v))

    activations(0, 0)
    gradients(0, 0, True)
    token_step(1, 1)
    token_step(1, -1)
    by_core(functools.partial(stage_d, 1))
    activations(0, 1)
    token_step(1, 2)
    token_step(1, -2)
    gradients(0, 1, False)
    token_step(1, 3)
    token_step(1, -3)
    token_step(1, 4)
    for c in range(CHUNKS):
        remote(hg.at[1, c], hg.at[1, c], h_s.at[c], h_r.at[c], dom=anti).wait_recv()
    token_side(1)
    activations(1, 0)
    gradients(1, 0, True)
    activations(1, 1)
    gradients(1, 1, False)

    for w in range(SHARED):
        for h in range(PIECES):
            for s in range(4):
                ring(w, s, h).wait_send()
            for s in range(3):
                ring(w, -s, h, 1).wait_send()
            for s in range(-3, 5):
                side(w, s, h).wait_send()
    swap().wait_send()
    for c in range(CHUNKS):
        swap_hg(c).wait_send()
        for kind in range(2):
            for o in (2, 1, 3):
                w1(c, kind, o).wait_send()

    def stage_e(axis):
        for c in range(CHUNKS):
            for i in range(4):
                w2(axis, c, i).wait_send()

    by_core(stage_e)

    def products(c):
        way_v = toward_pair(c)
        for w in range(SHARED):

            @pl.loop(1, 8)
            def _(i):
                u_, v_ = wrap(u - i // 2, SIDE), wrap(v + lax.rem(i, 2) * way_v, SIDE)
                if w == 0:
                    domain = at_uv(u_, v_)
                else:
                    domain = at_uv(wrap(u_ + 2, SIDE), wrap(v_ + 2, SIDE))
                here = stack.at[c, domain]
                remote(grads.at[w, c, i], here, g_s.at[w, c, i], g_r.at[w, c, i], dom=at_uv(u_, v_)).wait_send()
                remote(here, here, g_s.at[w, c, i], g_r.at[w, c, i], dom=at_uv(u_, v_)).wait_recv()

        @pl.loop(0, 2 * ROWS // 32)
        def _(r):
            at = pl.ds(pl.multiple_of(r * 32, 32), 32)
            total = scale[0] * stack[c, 0, at, :].astype(jnp.float32)
            for j in range(1, N_DOM):
                total += scale[j] * stack[c, j, at, :].astype(jnp.float32)
            mean[at, :] = total

        @pl.loop(0, N_DOM)
        def _(j):
            toward = jnp.zeros((8, 2 * LANES), jnp.float32)
            own = jnp.zeros((8, 2 * LANES), jnp.float32)
            for r in range(2 * ROWS // 32):
                at = pl.ds(r * 32, 32)
                g = stack[c, j, at, :].astype(jnp.float32)
                toward += jnp.sum((g * mean[at, :]).reshape(4, 8, 2 * LANES), axis=0)
                own += jnp.sum((g * g).reshape(4, 8, 2 * LANES), axis=0)
            toward = jnp.sum(toward, axis=0, keepdims=True)
            own = jnp.sum(own, axis=0, keepdims=True)
            part[j] += toward[:, :LANES] + toward[:, LANES:]
            part[N_DOM + j] += own[:, :LANES] + own[:, LANES:]

    for c in range(CHUNKS):
        products(c)

    group = lax.broadcasted_iota(jnp.int32, (8, LANES), 1) // 32
    packed = jnp.zeros((8, LANES), jnp.float32)
    sums = part[...].reshape(2 * N_DOM, LANES)
    for q in range(4):
        own = sums[8 * q : 8 * q + 8]
        own = own + pltpu.roll(own, 64, 1)
        own = own + pltpu.roll(own, 32, 1)
        packed = jnp.where(group == q, own, packed)
    msg[...] = packed
    ar1[me] = packed

    @pl.loop(1, N_DOM)
    def _(k):
        t = lax.rem(me + k, N_DOM)
        remote(msg, ar1.at[me], a1_s.at[t], a1_r.at[me], dom=t).start()

    @pl.loop(1, N_DOM)
    def _(k):
        t = lax.rem(me + k, N_DOM)
        remote(msg, ar1.at[t], a1_s.at[t], a1_r.at[t], dom=t).wait_recv()

    total = ar1[0]
    for j in range(1, N_DOM):
        total += ar1[j]
    msg2[...] = total
    ar2[f] = total

    @pl.loop(1, N_FSDP)
    def _(k):
        t = lax.rem(f + k, N_FSDP)
        remote(msg2, ar2.at[f], a2_s.at[t], a2_r.at[f], fsdp=t).start()

    @pl.loop(1, N_FSDP)
    def _(k):
        t = lax.rem(f + k, N_FSDP)
        remote(msg2, ar2.at[t], a2_s.at[t], a2_r.at[t], fsdp=t).wait_recv()

    total = ar2[0]
    for j in range(1, N_FSDP):
        total += ar2[j]
    for k in range(1, N_DOM):
        t = lax.rem(me + k, N_DOM)
        remote(msg, ar1.at[me], a1_s.at[t], a1_r.at[me], dom=t).wait_send()
        t = lax.rem(f + k, N_FSDP)
        remote(msg2, ar2.at[f], a2_s.at[t], a2_r.at[f], fsdp=t).wait_send()

    total = [jnp.sum(jnp.where(group == q, total, 0.0), axis=1, keepdims=True) for q in range(4)]
    toward, own = jnp.concatenate(total[:2], axis=0), jnp.concatenate(total[2:], axis=0)
    spread = jnp.sum(prior * toward, axis=0, keepdims=True)
    cosine = toward / jnp.sqrt((own + EPS) * (spread + EPS))
    scaled = prior * jnp.exp(STEP_SIZE * cosine)
    alpha = scaled / jnp.sum(scaled, axis=0, keepdims=True)
    row = lax.broadcasted_iota(jnp.int32, (N_DOM, N_DOM), 0)
    lane = lax.broadcasted_iota(jnp.int32, (N_DOM, N_DOM), 1)
    oa_ref[...] = jnp.sum(jnp.where(row == lane, alpha, 0.0), axis=0, keepdims=True)
    spread_out(alpha)

    def mixed(c, lo, r):
        at = pl.ds(pl.multiple_of(lo + r * 32, 32), 32)
        mix = scale[0] * stack[c, 0, at, :].astype(jnp.float32)
        for j in range(1, N_DOM):
            mix += scale[j] * stack[c, j, at, :].astype(jnp.float32)
        return mix

    def over(c):
        return remote(mix_s.at[c], mix_r.at[c], m_s.at[c], m_r.at[c], dom=near_v(-toward_pair(c)))

    for c in range(CHUNKS):

        @pl.loop(0, ROWS // 32)
        def _(r):
            mix_s[c, pl.ds(pl.multiple_of(r * 32, 32), 32), :] = mixed(c, ROWS, r)

        over(c).start()

    for c in range(CHUNKS):
        cols = columns(c, half(c, v))

        @pl.loop(0, ROWS // 32)
        def _(r):
            at = pl.ds(pl.multiple_of(r * 32, 32), 32)
            mix = mixed(c, 0, r)
            og_ref[at, cols] = mix[:, :LANES]
            ou_ref[at, cols] = mix[:, LANES:]

    for c in range(CHUNKS):
        cols = columns(c, 1 - half(c, v))
        over(c).wait_recv()
        og_ref[:, cols] = mix_r[c, :, :LANES]
        ou_ref[:, cols] = mix_r[c, :, LANES:]
    for c in range(CHUNKS):
        over(c).wait_send()


def local(tokens, hidden_grad, gate_weight, up_weight, counts):
    vmem = pl.BlockSpec(memory_space=pltpu.VMEM)
    dma = pltpu.SemaphoreType.DMA
    bf16, f32 = jnp.bfloat16, jnp.float32
    mix_gate, mix_up, alpha = pl.pallas_call(
        kernel,
        out_shape=(
            jax.ShapeDtypeStruct((ROWS, 4 * LANES), f32),
            jax.ShapeDtypeStruct((ROWS, 4 * LANES), f32),
            jax.ShapeDtypeStruct((1, N_DOM), f32),
        ),
        in_specs=[vmem] * 4 + [pl.BlockSpec(memory_space=pltpu.SMEM)],
        out_specs=(vmem,) * 3,
        scratch_shapes=[
            pltpu.VMEM((SHARED, CHUNKS, TOKENS, LANES), bf16),
            pltpu.VMEM((SHARED, TOKENS, D), bf16),
            pltpu.VMEM((SHARED, D, TOKENS), bf16),
            pltpu.VMEM((CHUNKS, 2, SIDE, SIDE, ROWS, LANES), bf16),
            pltpu.VMEM((SHARED, CHUNKS, 8, 2 * ROWS, 2 * LANES), bf16),
            pltpu.VMEM((CHUNKS, N_DOM, 2 * ROWS, 2 * LANES), bf16),
            pltpu.VMEM((TOKENS, 2 * LANES), bf16),
            pltpu.VMEM((2 * ROWS, 2 * LANES), f32),
            pltpu.VMEM((N_DOM, 1, 2 * LANES), f32),
            pltpu.VMEM((2 * N_DOM, 1, LANES), f32),
            pltpu.VMEM((8, LANES), f32),
            pltpu.VMEM((8, LANES), f32),
            pltpu.VMEM((N_DOM, 8, LANES), f32),
            pltpu.VMEM((N_FSDP, 8, LANES), f32),
            pltpu.VMEM((CHUNKS, ROWS, 2 * LANES), f32),
            pltpu.VMEM((CHUNKS, ROWS, 2 * LANES), f32),
            dma((SHARED, 7, PIECES)), dma((SHARED, 7, PIECES)), dma((SHARED, 8, PIECES)), dma((SHARED, 8, PIECES)),
            dma((1,)), dma((1,)), dma((CHUNKS,)), dma((CHUNKS,)),
            dma((CHUNKS, 2, 4)), dma((CHUNKS, 2, 4)), dma((CHUNKS, 4)), dma((CHUNKS, 4)),
            dma((SHARED, CHUNKS, 8)), dma((SHARED, CHUNKS, 8)),
            dma((N_DOM,)), dma((N_DOM,)), dma((N_FSDP,)), dma((N_FSDP,)), dma((CHUNKS,)), dma((CHUNKS,)),
        ],
        compiler_params=pltpu.CompilerParams(
            collective_id=0, has_side_effects=True, vmem_limit_bytes=60 * 2**20
        ),
        cost_estimate=pl.CostEstimate(flops=13 * 10**9, bytes_accessed=4 * 10**6, transcendentals=400000),
    )(tokens, hidden_grad, gate_weight, up_weight, counts)
    return mix_gate, mix_up, alpha.reshape(N_DOM)


def solution(mesh):
    return jax.shard_map(
        local,
        mesh=mesh,
        in_specs=(
            P("dom", "fsdp", None),
            P("dom", None, "fsdp"),
            P("dom", "fsdp"),
            P("dom", "fsdp"),
            P(),
        ),
        out_specs=(P("dom", "fsdp"), P("dom", "fsdp"), P()),
        check_vma=False,
    )
```

```python
import functools

import jax
import jax.numpy as jnp
from jax import lax
from jax.experimental import pallas as pl
from jax.experimental.pallas import tpu as pltpu
from jax.sharding import PartitionSpec as P

STEP_SIZE = 4.0
EPS = 1e-06
MESH = pl.DeviceIdType.MESH

SIDE = 4
N_DOM = 16
N_FSDP = 16
SHARED = 2
CHUNKS = 2
LANES = 128
ROWS = 256
TOK = 48
TOKENS = 768
D = 4096
PIECES = 2
PIECE = D // PIECES
ORDER = (5, 3, 7, 4, 2, 6, 1)


def wrap(i, n):
    return lax.rem(i + n, n)


def remote(src, dst, ss, rs, **where):
    return pltpu.make_async_remote_copy(
        src_ref=src, dst_ref=dst, send_sem=ss, recv_sem=rs, device_id=where, device_id_type=MESH
    )


def kernel(
    tok_ref, hg_ref, gw_ref, uw_ref, cnt_ref,
    og_ref, ou_ref, oa_ref,
    hg, tokens, tokens_t, weights, grads, stack, acts, mean, scale, part, msg, msg2, ar1, ar2, mix_s, mix_r,
    rs_s, rs_r, sb_s, sb_r, sw_s, sw_r, h_s, h_r, w1_s, w1_r, w2_s, w2_r, g_s, g_r, a1_s, a1_r, a2_s, a2_r, m_s, m_r,
):
    me = lax.axis_index("dom")
    x, y = me // SIDE, lax.rem(me, SIDE)
    f = lax.axis_index("fsdp")
    z, core = f // 2, lax.rem(f, 2)
    way = 1 - 2 * core
    sibling = f + way
    onward = wrap(z + way, 8) * 2 + core
    behind = wrap(z - way, 8) * 2 + core
    anti = wrap(x + 2, SIDE) * SIDE + wrap(y + 2, SIDE)
    u, v = x + core * (y - x), y + core * (x - y)

    def at_uv(u_, v_):
        return u_ * (4 - 3 * core) + v_ * (1 + 3 * core)

    def near_u(off):
        return at_uv(wrap(u + off, SIDE), v)

    def near_v(off):
        return at_uv(u, wrap(v + off, SIDE))

    def toward_pair(c):
        return 1 - 2 * lax.rem(v + c, 2)

    def half(c, v_):
        return lax.rem((v_ + c) // 2, 2)

    def columns(c, h):
        return pl.ds(pl.multiple_of((2 * c + h) * LANES, LANES), LANES)

    barrier = pltpu.get_barrier_semaphore()
    for where in (
        {"dom": near_u(1)},
        {"dom": near_u(-1)},
        {"dom": near_v(1)},
        {"dom": near_v(-1)},
        {"dom": near_v(2)},
        {"dom": anti},
        {"fsdp": onward},
        {"fsdp": behind},
        {"fsdp": sibling},
    ):
        pl.semaphore_signal(barrier, inc=1, device_id=where, device_id_type=MESH)
    pl.semaphore_wait(barrier, 9)

    def shard(w, s, c, h):
        owner = wrap(z - s * (1 - 2 * c) + 8, 8) * 2 + c
        return tokens.at[w, pl.ds(pl.multiple_of(owner * TOK, 16), TOK), pl.ds(h * PIECE, PIECE)]

    def source(w, s, h):
        if w == 0 and s == 0:
            return tok_ref.at[0, :, pl.ds(h * PIECE, PIECE)]
        return shard(w, s, core, h)

    def ring(w, s, h, back=0):
        i = 4 - s if back else s
        return remote(
            source(w, s, h), shard(w, s, core, h), rs_s.at[w, i, h], rs_r.at[w, i, h], fsdp=(onward, behind)[back]
        )

    def side(w, s, h):
        return remote(source(w, s, h), shard(w, s, core, h), sb_s.at[w, s + 3, h], sb_r.at[w, s + 3, h], fsdp=sibling)

    def token_start(w):
        for h in range(PIECES):
            ring(w, 0, h).start()
            ring(w, 0, h, 1).start()

    def token_step(w, s):
        for h in range(PIECES):
            here = shard(w, s, core, h)
            i = s - 1 if s > 0 else 3 - s
            remote(here, here, rs_s.at[w, i, h], rs_r.at[w, i, h], fsdp=onward).wait_recv()
            if 0 < s < 4:
                ring(w, s, h).start()
            if -3 < s < 0:
                ring(w, s, h, 1).start()
            side(w, s, h).start()

    def token_side(w):
        @pl.loop(0, 8)
        def _(s):
            for h in range(PIECES):
                here = shard(w, s - 3, 1 - core, h)
                remote(here, here, sb_s.at[w, s, h], sb_r.at[w, s, h], fsdp=sibling).wait_recv()

    own_rows = pl.ds(pl.multiple_of(f * TOK, 16), TOK)

    def swap():
        return remote(tok_ref.at[0], tokens.at[1, own_rows], sw_s.at[0], sw_r.at[0], dom=anti)

    def swap_hg(c):
        return remote(hg_ref.at[0, :, columns(c, 1 - half(c, v))], hg.at[1, c], h_s.at[c], h_r.at[c], dom=anti)

    def w1(c, kind, o):
        to = wrap(v + o, SIDE)
        src = (gw_ref, uw_ref)[kind].at[:, columns(c, half(c, to))]
        return remote(src, weights.at[c, kind, x, y], w1_s.at[c, kind, o], w1_r.at[c, kind, o], dom=at_uv(u, to))

    def w1_got(c, kind, o):
        d = near_v(-o)
        here = weights.at[c, kind, d // SIDE, lax.rem(d, SIDE)]
        remote(here, here, w1_s.at[c, kind, o], w1_r.at[c, kind, o], dom=d).wait_recv()

    MID = ROWS // 2

    def line(axis, c, off, lo=0, n=ROWS):
        at = wrap(u + off, SIDE)
        if axis == 0:
            return weights.at[c, :, at, :, pl.ds(lo, n)]
        return weights.at[c, :, :, at, pl.ds(lo, n)]

    def w2(axis, c, i):
        to = (1, -1)[i % 2]
        src = line(axis, c, 0) if i < 2 else line(axis, c, -to, (i - 2) * MID, MID)
        return remote(src, src, w2_s.at[c, i], w2_r.at[c, i], dom=near_u(to))

    def w2_got(axis, c, i):
        to = (1, -1)[i % 2]
        here = line(axis, c, -to) if i < 2 else line(axis, c, 2, (i - 2) * MID, MID)
        remote(here, here, w2_s.at[c, i], w2_r.at[c, i], dom=near_u(to)).wait_recv()

    def by_core(do):
        for axis in range(2):
            pl.when(core == axis)(functools.partial(do, axis))

    def stage_b(c, axis):
        for i in range(2):
            w2(axis, c, i).start()

    def stage_c(c, axis):
        for i in range(2):
            w2_got(axis, c, i)
            w2(axis, c, i + 2).start()

    def stage_d(c, axis):
        for i in range(2, 4):
            w2_got(axis, c, i)

    token_start(0)
    swap().start()
    for c in range(CHUNKS):
        for kind in range(2):
            for o in (2, 1, 3):
                w1(c, kind, o).start()
    for h in range(PIECES):
        side(0, 0, h).start()

    tokens[0, own_rows, :] = tok_ref[0]
    for c in range(CHUNKS):
        cols = columns(c, half(c, v))
        weights[c, 0, x, y] = gw_ref[:, cols]
        weights[c, 1, x, y] = uw_ref[:, cols]
        hg[0, c] = hg_ref[0, :, cols]

    def spread_out(column):
        for j in range(N_DOM):
            scale[j] = jnp.broadcast_to(column[j : j + 1, :], (1, 2 * LANES))

    count = cnt_ref[0]
    for j in range(1, N_DOM):
        count += cnt_ref[j]
    count = jnp.full((1, 2 * LANES), count.astype(jnp.float32))
    for j in range(N_DOM):
        scale[j] = jnp.full((1, 2 * LANES), cnt_ref[j].astype(jnp.float32)) / count
    prior = scale[...].reshape(N_DOM, 2 * LANES)[:, :1]
    part[...] = jnp.zeros_like(part)

    for c in range(CHUNKS):
        for kind in range(2):
            for o in (2, 1, 3):
                w1_got(c, kind, o)
        by_core(functools.partial(stage_b, c))
    for c in range(CHUNKS):
        swap_hg(c).start()
    token_step(0, 1)
    token_step(0, -1)
    token_step(0, 2)
    token_step(0, -2)
    by_core(functools.partial(stage_c, 0))
    token_step(0, 3)
    token_step(0, -3)
    by_core(functools.partial(stage_c, 1))
    token_step(0, 4)
    remote(tokens.at[1, own_rows], tokens.at[1, own_rows], sw_s.at[0], sw_r.at[0], dom=anti).wait_recv()
    token_start(1)
    for h in range(PIECES):
        side(1, 0, h).start()
    token_side(0)
    by_core(functools.partial(stage_d, 0))

    def activations(w, c):
        @pl.loop(0, TOKENS // 256)
        def _(m):
            at = pl.ds(pl.multiple_of(m * 256, 256), 256)
            wide = jnp.concatenate([weights[c, 0].reshape(D, LANES), weights[c, 1].reshape(D, LANES)], axis=1)
            pre = jnp.dot(tokens[w, at, :], wide, preferred_element_type=jnp.float32)
            gate, up = pre[:, :LANES], pre[:, LANES:]
            g = hg[w, c, at, :].astype(jnp.float32)
            s = jax.nn.sigmoid(gate)
            acts[at, :LANES] = (g * up * s * (1.0 + gate * (1.0 - s))).astype(jnp.bfloat16)
            acts[at, LANES:] = (g * gate * s).astype(jnp.bfloat16)

    def gradients(w, c, turn):
        way_v = toward_pair(c)
        domain = (me, anti)[w]

        def block_of(d):
            rows = pl.ds(pl.multiple_of(d * ROWS, ROWS), ROWS)
            if turn:
                tokens_t[w, rows, :] = tokens[w, :, rows].T
            out = jnp.dot(tokens_t[w, rows, :], acts[...], preferred_element_type=jnp.float32)
            return out.astype(jnp.bfloat16)

        @pl.loop(0, 7)
        def _(k):
            i = ORDER[0]
            for n in range(1, 7):
                i = jnp.where(k == n, ORDER[n], i)
            du, pair = i // 2, lax.rem(i, 2)
            u_ = wrap(u + du, SIDE)
            first = wrap(v + pair * way_v, SIDE)
            grads[w, c, i, :ROWS, :] = block_of(at_uv(u_, first))
            grads[w, c, i, ROWS:, :] = block_of(at_uv(u_, wrap(v - way_v + 3 * pair * way_v + 4, SIDE)))
            remote(
                grads.at[w, c, i], stack.at[c, domain], g_s.at[w, c, i], g_r.at[w, c, i], dom=at_uv(u_, first)
            ).start()

        stack[c, domain, :ROWS, :] = block_of(me)
        stack[c, domain, ROWS:, :] = block_of(near_v(-way_v))

    activations(0, 0)
    gradients(0, 0, True)
    token_step(1, 1)
    token_step(1, -1)
    by_core(functools.partial(stage_d, 1))
    activations(0, 1)
    token_step(1, 2)
    token_step(1, -2)
    gradients(0, 1, False)
    token_step(1, 3)
    token_step(1, -3)
    token_step(1, 4)
    for c in range(CHUNKS):
        remote(hg.at[1, c], hg.at[1, c], h_s.at[c], h_r.at[c], dom=anti).wait_recv()
    token_side(1)
    activations(1, 0)
    gradients(1, 0, True)
    activations(1, 1)
    gradients(1, 1, False)

    for w in range(SHARED):
        for h in range(PIECES):
            for s in range(4):
                ring(w, s, h).wait_send()
            for s in range(3):
                ring(w, -s, h, 1).wait_send()
            for s in range(-3, 5):
                side(w, s, h).wait_send()
    swap().wait_send()
    for c in range(CHUNKS):
        swap_hg(c).wait_send()
        for kind in range(2):
            for o in (2, 1, 3):
                w1(c, kind, o).wait_send()

    def stage_e(axis):
        for c in range(CHUNKS):
            for i in range(4):
                w2(axis, c, i).wait_send()

    by_core(stage_e)

    def products(c):
        way_v = toward_pair(c)
        for w in range(SHARED):

            @pl.loop(1, 8)
            def _(i):
                u_, v_ = wrap(u - i // 2, SIDE), wrap(v + lax.rem(i, 2) * way_v, SIDE)
                if w == 0:
                    domain = at_uv(u_, v_)
                else:
                    domain = at_uv(wrap(u_ + 2, SIDE), wrap(v_ + 2, SIDE))
                here = stack.at[c, domain]
                remote(grads.at[w, c, i], here, g_s.at[w, c, i], g_r.at[w, c, i], dom=at_uv(u_, v_)).wait_send()
                remote(here, here, g_s.at[w, c, i], g_r.at[w, c, i], dom=at_uv(u_, v_)).wait_recv()

        @pl.loop(0, 2 * ROWS // 32)
        def _(r):
            at = pl.ds(pl.multiple_of(r * 32, 32), 32)
            total = scale[0] * stack[c, 0, at, :].astype(jnp.float32)
            for j in range(1, N_DOM):
                total += scale[j] * stack[c, j, at, :].astype(jnp.float32)
            mean[at, :] = total

        @pl.loop(0, N_DOM)
        def _(j):
            toward = jnp.zeros((8, 2 * LANES), jnp.float32)
            own = jnp.zeros((8, 2 * LANES), jnp.float32)
            for r in range(2 * ROWS // 32):
                at = pl.ds(r * 32, 32)
                g = stack[c, j, at, :].astype(jnp.float32)
                toward += jnp.sum((g * mean[at, :]).reshape(4, 8, 2 * LANES), axis=0)
                own += jnp.sum((g * g).reshape(4, 8, 2 * LANES), axis=0)
            toward = jnp.sum(toward, axis=0, keepdims=True)
            own = jnp.sum(own, axis=0, keepdims=True)
            part[j] += toward[:, :LANES] + toward[:, LANES:]
            part[N_DOM + j] += own[:, :LANES] + own[:, LANES:]

    for c in range(CHUNKS):
        products(c)

    group = lax.broadcasted_iota(jnp.int32, (8, LANES), 1) // 32
    packed = jnp.zeros((8, LANES), jnp.float32)
    sums = part[...].reshape(2 * N_DOM, LANES)
    for q in range(4):
        own = sums[8 * q : 8 * q + 8]
        own = own + pltpu.roll(own, 64, 1)
        own = own + pltpu.roll(own, 32, 1)
        packed = jnp.where(group == q, own, packed)
    msg[...] = packed
    ar1[me] = packed

    @pl.loop(1, N_DOM)
    def _(k):
        t = lax.rem(me + k, N_DOM)
        remote(msg, ar1.at[me], a1_s.at[t], a1_r.at[me], dom=t).start()

    @pl.loop(1, N_DOM)
    def _(k):
        t = lax.rem(me + k, N_DOM)
        remote(msg, ar1.at[t], a1_s.at[t], a1_r.at[t], dom=t).wait_recv()

    total = ar1[0]
    for j in range(1, N_DOM):
        total += ar1[j]
    msg2[...] = total
    ar2[f] = total

    @pl.loop(1, N_FSDP)
    def _(k):
        t = lax.rem(f + k, N_FSDP)
        remote(msg2, ar2.at[f], a2_s.at[t], a2_r.at[f], fsdp=t).start()

    @pl.loop(1, N_FSDP)
    def _(k):
        t = lax.rem(f + k, N_FSDP)
        remote(msg2, ar2.at[t], a2_s.at[t], a2_r.at[t], fsdp=t).wait_recv()

    total = ar2[0]
    for j in range(1, N_FSDP):
        total += ar2[j]
    for k in range(1, N_DOM):
        t = lax.rem(me + k, N_DOM)
        remote(msg, ar1.at[me], a1_s.at[t], a1_r.at[me], dom=t).wait_send()
        t = lax.rem(f + k, N_FSDP)
        remote(msg2, ar2.at[f], a2_s.at[t], a2_r.at[f], fsdp=t).wait_send()

    total = [jnp.sum(jnp.where(group == q, total, 0.0), axis=1, keepdims=True) for q in range(4)]
    toward, own = jnp.concatenate(total[:2], axis=0), jnp.concatenate(total[2:], axis=0)
    spread = jnp.sum(prior * toward, axis=0, keepdims=True)
    cosine = toward / jnp.sqrt((own + EPS) * (spread + EPS))
    scaled = prior * jnp.exp(STEP_SIZE * cosine)
    alpha = scaled / jnp.sum(scaled, axis=0, keepdims=True)
    row = lax.broadcasted_iota(jnp.int32, (N_DOM, N_DOM), 0)
    lane = lax.broadcasted_iota(jnp.int32, (N_DOM, N_DOM), 1)
    oa_ref[...] = jnp.sum(jnp.where(row == lane, alpha, 0.0), axis=0, keepdims=True)
    spread_out(alpha)

    def mixed(c, lo, r):
        at = pl.ds(pl.multiple_of(lo + r * 32, 32), 32)
        mix = scale[0] * stack[c, 0, at, :].astype(jnp.float32)
        for j in range(1, N_DOM):
            mix += scale[j] * stack[c, j, at, :].astype(jnp.float32)
        return mix

    def over(c):
        return remote(mix_s.at[c], mix_r.at[c], m_s.at[c], m_r.at[c], dom=near_v(-toward_pair(c)))

    for c in range(CHUNKS):

        @pl.loop(0, ROWS // 32)
        def _(r):
            mix_s[c, pl.ds(pl.multiple_of(r * 32, 32), 32), :] = mixed(c, ROWS, r)

        over(c).start()

    for c in range(CHUNKS):
        cols = columns(c, half(c, v))

        @pl.loop(0, ROWS // 32)
        def _(r):
            at = pl.ds(pl.multiple_of(r * 32, 32), 32)
            mix = mixed(c, 0, r)
            og_ref[at, cols] = mix[:, :LANES]
            ou_ref[at, cols] = mix[:, LANES:]

    for c in range(CHUNKS):
        cols = columns(c, 1 - half(c, v))
        over(c).wait_recv()
        og_ref[:, cols] = mix_r[c, :, :LANES]
        ou_ref[:, cols] = mix_r[c, :, LANES:]
    for c in range(CHUNKS):
        over(c).wait_send()


def local(tokens, hidden_grad, gate_weight, up_weight, counts):
    vmem = pl.BlockSpec(memory_space=pltpu.VMEM)
    dma = pltpu.SemaphoreType.DMA
    bf16, f32 = jnp.bfloat16, jnp.float32
    mix_gate, mix_up, alpha = pl.pallas_call(
        kernel,
        out_shape=(
            jax.ShapeDtypeStruct((ROWS, 4 * LANES), f32),
            jax.ShapeDtypeStruct((ROWS, 4 * LANES), f32),
            jax.ShapeDtypeStruct((1, N_DOM), f32),
        ),
        in_specs=[vmem] * 4 + [pl.BlockSpec(memory_space=pltpu.SMEM)],
        out_specs=(vmem,) * 3,
        scratch_shapes=[
            pltpu.VMEM((SHARED, CHUNKS, TOKENS, LANES), bf16),
            pltpu.VMEM((SHARED, TOKENS, D), bf16),
            pltpu.VMEM((SHARED, D, TOKENS), bf16),
            pltpu.VMEM((CHUNKS, 2, SIDE, SIDE, ROWS, LANES), bf16),
            pltpu.VMEM((SHARED, CHUNKS, 8, 2 * ROWS, 2 * LANES), bf16),
            pltpu.VMEM((CHUNKS, N_DOM, 2 * ROWS, 2 * LANES), bf16),
            pltpu.VMEM((TOKENS, 2 * LANES), bf16),
            pltpu.VMEM((2 * ROWS, 2 * LANES), f32),
            pltpu.VMEM((N_DOM, 1, 2 * LANES), f32),
            pltpu.VMEM((2 * N_DOM, 1, LANES), f32),
            pltpu.VMEM((8, LANES), f32),
            pltpu.VMEM((8, LANES), f32),
            pltpu.VMEM((N_DOM, 8, LANES), f32),
            pltpu.VMEM((N_FSDP, 8, LANES), f32),
            pltpu.VMEM((CHUNKS, ROWS, 2 * LANES), f32),
            pltpu.VMEM((CHUNKS, ROWS, 2 * LANES), f32),
            dma((SHARED, 7, PIECES)), dma((SHARED, 7, PIECES)), dma((SHARED, 8, PIECES)), dma((SHARED, 8, PIECES)),
            dma((1,)), dma((1,)), dma((CHUNKS,)), dma((CHUNKS,)),
            dma((CHUNKS, 2, 4)), dma((CHUNKS, 2, 4)), dma((CHUNKS, 4)), dma((CHUNKS, 4)),
            dma((SHARED, CHUNKS, 8)), dma((SHARED, CHUNKS, 8)),
            dma((N_DOM,)), dma((N_DOM,)), dma((N_FSDP,)), dma((N_FSDP,)), dma((CHUNKS,)), dma((CHUNKS,)),
        ],
        compiler_params=pltpu.CompilerParams(
            collective_id=0, has_side_effects=True, vmem_limit_bytes=60 * 2**20
        ),
        cost_estimate=pl.CostEstimate(flops=13 * 10**9, bytes_accessed=4 * 10**6, transcendentals=400000),
    )(tokens, hidden_grad, gate_weight, up_weight, counts)
    return mix_gate, mix_up, alpha.reshape(N_DOM)


def solution(mesh):
    return jax.shard_map(
        local,
        mesh=mesh,
        in_specs=(
            P("dom", "fsdp", None),
            P("dom", None, "fsdp"),
            P("dom", "fsdp"),
            P("dom", "fsdp"),
            P(),
        ),
        out_specs=(P("dom", "fsdp"), P("dom", "fsdp"), P()),
        check_vma=False,
    )
```

```python
import functools

import jax
import jax.numpy as jnp
from jax import lax
from jax.experimental import pallas as pl
from jax.experimental.pallas import tpu as pltpu
from jax.sharding import PartitionSpec as P

STEP_SIZE = 4.0
EPS = 1e-06
MESH = pl.DeviceIdType.MESH

SIDE = 4
N_DOM = 16
N_FSDP = 16
SHARED = 2
CHUNKS = 2
LANES = 128
ROWS = 256
TOK = 48
TOKENS = 768
D = 4096
PIECES = 2
PIECE = D // PIECES
ORDER = (5, 3, 7, 4, 2, 6, 1)


def wrap(i, n):
    return lax.rem(i + n, n)


def remote(src, dst, ss, rs, **where):
    return pltpu.make_async_remote_copy(
        src_ref=src, dst_ref=dst, send_sem=ss, recv_sem=rs, device_id=where, device_id_type=MESH
    )


def kernel(
    tok_ref, hg_ref, gw_ref, uw_ref, cnt_ref,
    og_ref, ou_ref, oa_ref,
    hg, tokens, tokens_t, weights, grads, stack, acts, mean, scale, part, msg, msg2, ar1, ar2, mix_s, mix_r,
    rs_s, rs_r, sb_s, sb_r, sw_s, sw_r, h_s, h_r, w1_s, w1_r, w2_s, w2_r, g_s, g_r, a1_s, a1_r, a2_s, a2_r, m_s, m_r,
):
    me = lax.axis_index("dom")
    x, y = me // SIDE, lax.rem(me, SIDE)
    f = lax.axis_index("fsdp")
    z, core = f // 2, lax.rem(f, 2)
    way = 1 - 2 * core
    sibling = f + way
    onward = wrap(z + way, 8) * 2 + core
    behind = wrap(z - way, 8) * 2 + core
    anti = wrap(x + 2, SIDE) * SIDE + wrap(y + 2, SIDE)
    u, v = x + core * (y - x), y + core * (x - y)

    def at_uv(u_, v_):
        return u_ * (4 - 3 * core) + v_ * (1 + 3 * core)

    def near_u(off):
        return at_uv(wrap(u + off, SIDE), v)

    def near_v(off):
        return at_uv(u, wrap(v + off, SIDE))

    def toward_pair(c):
        return 1 - 2 * lax.rem(v + c, 2)

    def half(c, v_):
        return lax.rem((v_ + c) // 2, 2)

    def columns(c, h):
        return pl.ds(pl.multiple_of((2 * c + h) * LANES, LANES), LANES)

    barrier = pltpu.get_barrier_semaphore()
    for where in (
        {"dom": near_u(1)},
        {"dom": near_u(-1)},
        {"dom": near_v(1)},
        {"dom": near_v(-1)},
        {"dom": near_v(2)},
        {"dom": anti},
        {"fsdp": onward},
        {"fsdp": behind},
        {"fsdp": sibling},
    ):
        pl.semaphore_signal(barrier, inc=1, device_id=where, device_id_type=MESH)
    pl.semaphore_wait(barrier, 9)

    def shard(w, s, c, h):
        owner = wrap(z - s * (1 - 2 * c) + 8, 8) * 2 + c
        return tokens.at[w, pl.ds(pl.multiple_of(owner * TOK, 16), TOK), pl.ds(h * PIECE, PIECE)]

    def source(w, s, h):
        if w == 0 and s == 0:
            return tok_ref.at[0, :, pl.ds(h * PIECE, PIECE)]
        return shard(w, s, core, h)

    def ring(w, s, h, back=0):
        i = 4 - s if back else s
        return remote(
            source(w, s, h), shard(w, s, core, h), rs_s.at[w, i, h], rs_r.at[w, i, h], fsdp=(onward, behind)[back]
        )

    def side(w, s, h):
        return remote(source(w, s, h), shard(w, s, core, h), sb_s.at[w, s + 3, h], sb_r.at[w, s + 3, h], fsdp=sibling)

    def token_start(w):
        for h in range(PIECES):
            ring(w, 0, h).start()
            ring(w, 0, h, 1).start()

    def token_step(w, s):
        for h in range(PIECES):
            here = shard(w, s, core, h)
            i = s - 1 if s > 0 else 3 - s
            remote(here, here, rs_s.at[w, i, h], rs_r.at[w, i, h], fsdp=onward).wait_recv()
            if 0 < s < 4:
                ring(w, s, h).start()
            if -3 < s < 0:
                ring(w, s, h, 1).start()
            side(w, s, h).start()

    def token_side(w):
        @pl.loop(0, 8)
        def _(s):
            for h in range(PIECES):
                here = shard(w, s - 3, 1 - core, h)
                remote(here, here, sb_s.at[w, s, h], sb_r.at[w, s, h], fsdp=sibling).wait_recv()

    own_rows = pl.ds(pl.multiple_of(f * TOK, 16), TOK)

    def swap():
        return remote(tok_ref.at[0], tokens.at[1, own_rows], sw_s.at[0], sw_r.at[0], dom=anti)

    def swap_hg(c):
        return remote(hg_ref.at[0, :, columns(c, 1 - half(c, v))], hg.at[1, c], h_s.at[c], h_r.at[c], dom=anti)

    def w1(c, kind, o):
        to = wrap(v + o, SIDE)
        src = (gw_ref, uw_ref)[kind].at[:, columns(c, half(c, to))]
        return remote(src, weights.at[c, kind, x, y], w1_s.at[c, kind, o], w1_r.at[c, kind, o], dom=at_uv(u, to))

    def w1_got(c, kind, o):
        d = near_v(-o)
        here = weights.at[c, kind, d // SIDE, lax.rem(d, SIDE)]
        remote(here, here, w1_s.at[c, kind, o], w1_r.at[c, kind, o], dom=d).wait_recv()

    MID = ROWS // 2

    def line(axis, c, off, lo=0, n=ROWS):
        at = wrap(u + off, SIDE)
        if axis == 0:
            return weights.at[c, :, at, :, pl.ds(lo, n)]
        return weights.at[c, :, :, at, pl.ds(lo, n)]

    def w2(axis, c, i):
        to = (1, -1)[i % 2]
        src = line(axis, c, 0) if i < 2 else line(axis, c, -to, (i - 2) * MID, MID)
        return remote(src, src, w2_s.at[c, i], w2_r.at[c, i], dom=near_u(to))

    def w2_got(axis, c, i):
        to = (1, -1)[i % 2]
        here = line(axis, c, -to) if i < 2 else line(axis, c, 2, (i - 2) * MID, MID)
        remote(here, here, w2_s.at[c, i], w2_r.at[c, i], dom=near_u(to)).wait_recv()

    def by_core(do):
        for axis in range(2):
            pl.when(core == axis)(functools.partial(do, axis))

    def stage_b(c, axis):
        for i in range(2):
            w2(axis, c, i).start()

    def stage_c(c, axis):
        for i in range(2):
            w2_got(axis, c, i)
            w2(axis, c, i + 2).start()

    def stage_d(c, axis):
        for i in range(2, 4):
            w2_got(axis, c, i)

    token_start(0)
    swap().start()
    for c in range(CHUNKS):
        for kind in range(2):
            for o in (2, 1, 3):
                w1(c, kind, o).start()
    for h in range(PIECES):
        side(0, 0, h).start()

    tokens[0, own_rows, :] = tok_ref[0]
    for c in range(CHUNKS):
        cols = columns(c, half(c, v))
        weights[c, 0, x, y] = gw_ref[:, cols]
        weights[c, 1, x, y] = uw_ref[:, cols]
        hg[0, c] = hg_ref[0, :, cols]

    def spread_out(column):
        for j in range(N_DOM):
            scale[j] = jnp.broadcast_to(column[j : j + 1, :], (1, 2 * LANES))

    count = cnt_ref[0]
    for j in range(1, N_DOM):
        count += cnt_ref[j]
    count = jnp.full((1, 2 * LANES), count.astype(jnp.float32))
    for j in range(N_DOM):
        scale[j] = jnp.full((1, 2 * LANES), cnt_ref[j].astype(jnp.float32)) / count
    prior = scale[...].reshape(N_DOM, 2 * LANES)[:, :1]
    part[...] = jnp.zeros_like(part)

    for c in range(CHUNKS):
        for kind in range(2):
            for o in (2, 1, 3):
                w1_got(c, kind, o)
        by_core(functools.partial(stage_b, c))
    for c in range(CHUNKS):
        swap_hg(c).start()
    token_step(0, 1)
    token_step(0, -1)
    token_step(0, 2)
    token_step(0, -2)
    by_core(functools.partial(stage_c, 0))
    token_step(0, 3)
    token_step(0, -3)
    by_core(functools.partial(stage_c, 1))
    token_step(0, 4)
    remote(tokens.at[1, own_rows], tokens.at[1, own_rows], sw_s.at[0], sw_r.at[0], dom=anti).wait_recv()
    token_start(1)
    for h in range(PIECES):
        side(1, 0, h).start()
    token_side(0)
    by_core(functools.partial(stage_d, 0))

    def activations(w, c):
        @pl.loop(0, TOKENS // 256)
        def _(m):
            at = pl.ds(pl.multiple_of(m * 256, 256), 256)
            wide = jnp.concatenate([weights[c, 0].reshape(D, LANES), weights[c, 1].reshape(D, LANES)], axis=1)
            pre = jnp.dot(tokens[w, at, :], wide, preferred_element_type=jnp.float32)
            gate, up = pre[:, :LANES], pre[:, LANES:]
            g = hg[w, c, at, :].astype(jnp.float32)
            s = jax.nn.sigmoid(gate)
            acts[at, :LANES] = (g * up * s * (1.0 + gate * (1.0 - s))).astype(jnp.bfloat16)
            acts[at, LANES:] = (g * gate * s).astype(jnp.bfloat16)

    def gradients(w, c, turn):
        way_v = toward_pair(c)
        domain = (me, anti)[w]

        def block_of(d):
            rows = pl.ds(pl.multiple_of(d * ROWS, ROWS), ROWS)
            if turn:
                tokens_t[w, rows, :] = tokens[w, :, rows].T
            out = jnp.dot(tokens_t[w, rows, :], acts[...], preferred_element_type=jnp.float32)
            return out.astype(jnp.bfloat16)

        @pl.loop(0, 7)
        def _(k):
            i = ORDER[0]
            for n in range(1, 7):
                i = jnp.where(k == n, ORDER[n], i)
            du, pair = i // 2, lax.rem(i, 2)
            u_ = wrap(u + du, SIDE)
            first = wrap(v + pair * way_v, SIDE)
            grads[w, c, i, :ROWS, :] = block_of(at_uv(u_, first))
            grads[w, c, i, ROWS:, :] = block_of(at_uv(u_, wrap(v - way_v + 3 * pair * way_v + 4, SIDE)))
            remote(
                grads.at[w, c, i], stack.at[c, domain], g_s.at[w, c, i], g_r.at[w, c, i], dom=at_uv(u_, first)
            ).start()

        stack[c, domain, :ROWS, :] = block_of(me)
        stack[c, domain, ROWS:, :] = block_of(near_v(-way_v))

    activations(0, 0)
    gradients(0, 0, True)
    token_step(1, 1)
    token_step(1, -1)
    by_core(functools.partial(stage_d, 1))
    activations(0, 1)
    gradients(0, 1, False)
    token_step(1, 2)
    token_step(1, -2)
    token_step(1, 3)
    token_step(1, -3)
    token_step(1, 4)
    for c in range(CHUNKS):
        remote(hg.at[1, c], hg.at[1, c], h_s.at[c], h_r.at[c], dom=anti).wait_recv()
    token_side(1)
    activations(1, 0)
    gradients(1, 0, True)
    activations(1, 1)
    gradients(1, 1, False)

    for w in range(SHARED):
        for h in range(PIECES):
            for s in range(4):
                ring(w, s, h).wait_send()
            for s in range(3):
                ring(w, -s, h, 1).wait_send()
            for s in range(-3, 5):
                side(w, s, h).wait_send()
    swap().wait_send()
    for c in range(CHUNKS):
        swap_hg(c).wait_send()
        for kind in range(2):
            for o in (2, 1, 3):
                w1(c, kind, o).wait_send()

    def stage_e(axis):
        for c in range(CHUNKS):
            for i in range(4):
                w2(axis, c, i).wait_send()

    by_core(stage_e)

    def products(c):
        way_v = toward_pair(c)
        for w in range(SHARED):

            @pl.loop(1, 8)
            def _(i):
                u_, v_ = wrap(u - i // 2, SIDE), wrap(v + lax.rem(i, 2) * way_v, SIDE)
                if w == 0:
                    domain = at_uv(u_, v_)
                else:
                    domain = at_uv(wrap(u_ + 2, SIDE), wrap(v_ + 2, SIDE))
                here = stack.at[c, domain]
                remote(grads.at[w, c, i], here, g_s.at[w, c, i], g_r.at[w, c, i], dom=at_uv(u_, v_)).wait_send()
                remote(here, here, g_s.at[w, c, i], g_r.at[w, c, i], dom=at_uv(u_, v_)).wait_recv()

        @pl.loop(0, 2 * ROWS // 32)
        def _(r):
            at = pl.ds(pl.multiple_of(r * 32, 32), 32)
            total = scale[0] * stack[c, 0, at, :].astype(jnp.float32)
            for j in range(1, N_DOM):
                total += scale[j] * stack[c, j, at, :].astype(jnp.float32)
            mean[at, :] = total

        @pl.loop(0, N_DOM)
        def _(j):
            toward = jnp.zeros((8, 2 * LANES), jnp.float32)
            own = jnp.zeros((8, 2 * LANES), jnp.float32)
            for r in range(2 * ROWS // 32):
                at = pl.ds(r * 32, 32)
                g = stack[c, j, at, :].astype(jnp.float32)
                toward += jnp.sum((g * mean[at, :]).reshape(4, 8, 2 * LANES), axis=0)
                own += jnp.sum((g * g).reshape(4, 8, 2 * LANES), axis=0)
            toward = jnp.sum(toward, axis=0, keepdims=True)
            own = jnp.sum(own, axis=0, keepdims=True)
            part[j] += toward[:, :LANES] + toward[:, LANES:]
            part[N_DOM + j] += own[:, :LANES] + own[:, LANES:]

    for c in range(CHUNKS):
        products(c)

    group = lax.broadcasted_iota(jnp.int32, (8, LANES), 1) // 32
    packed = jnp.zeros((8, LANES), jnp.float32)
    sums = part[...].reshape(2 * N_DOM, LANES)
    for q in range(4):
        own = sums[8 * q : 8 * q + 8]
        own = own + pltpu.roll(own, 64, 1)
        own = own + pltpu.roll(own, 32, 1)
        packed = jnp.where(group == q, own, packed)
    msg[...] = packed
    ar1[me] = packed

    @pl.loop(1, N_DOM)
    def _(k):
        t = lax.rem(me + k, N_DOM)
        remote(msg, ar1.at[me], a1_s.at[t], a1_r.at[me], dom=t).start()

    @pl.loop(1, N_DOM)
    def _(k):
        t = lax.rem(me + k, N_DOM)
        remote(msg, ar1.at[t], a1_s.at[t], a1_r.at[t], dom=t).wait_recv()

    total = ar1[0]
    for j in range(1, N_DOM):
        total += ar1[j]
    msg2[...] = total
    ar2[f] = total

    @pl.loop(1, N_FSDP)
    def _(k):
        t = lax.rem(f + k, N_FSDP)
        remote(msg2, ar2.at[f], a2_s.at[t], a2_r.at[f], fsdp=t).start()

    @pl.loop(1, N_FSDP)
    def _(k):
        t = lax.rem(f + k, N_FSDP)
        remote(msg2, ar2.at[t], a2_s.at[t], a2_r.at[t], fsdp=t).wait_recv()

    total = ar2[0]
    for j in range(1, N_FSDP):
        total += ar2[j]
    for k in range(1, N_DOM):
        t = lax.rem(me + k, N_DOM)
        remote(msg, ar1.at[me], a1_s.at[t], a1_r.at[me], dom=t).wait_send()
        t = lax.rem(f + k, N_FSDP)
        remote(msg2, ar2.at[f], a2_s.at[t], a2_r.at[f], fsdp=t).wait_send()

    total = [jnp.sum(jnp.where(group == q, total, 0.0), axis=1, keepdims=True) for q in range(4)]
    toward, own = jnp.concatenate(total[:2], axis=0), jnp.concatenate(total[2:], axis=0)
    spread = jnp.sum(prior * toward, axis=0, keepdims=True)
    cosine = toward / jnp.sqrt((own + EPS) * (spread + EPS))
    scaled = prior * jnp.exp(STEP_SIZE * cosine)
    alpha = scaled / jnp.sum(scaled, axis=0, keepdims=True)
    row = lax.broadcasted_iota(jnp.int32, (N_DOM, N_DOM), 0)
    lane = lax.broadcasted_iota(jnp.int32, (N_DOM, N_DOM), 1)
    oa_ref[...] = jnp.sum(jnp.where(row == lane, alpha, 0.0), axis=0, keepdims=True)
    spread_out(alpha)

    def mixed(c, lo, r):
        at = pl.ds(pl.multiple_of(lo + r * 32, 32), 32)
        mix = scale[0] * stack[c, 0, at, :].astype(jnp.float32)
        for j in range(1, N_DOM):
            mix += scale[j] * stack[c, j, at, :].astype(jnp.float32)
        return mix

    def over(c):
        return remote(mix_s.at[c], mix_r.at[c], m_s.at[c], m_r.at[c], dom=near_v(-toward_pair(c)))

    for c in range(CHUNKS):

        @pl.loop(0, ROWS // 32)
        def _(r):
            mix_s[c, pl.ds(pl.multiple_of(r * 32, 32), 32), :] = mixed(c, ROWS, r)

        over(c).start()

    for c in range(CHUNKS):
        cols = columns(c, half(c, v))

        @pl.loop(0, ROWS // 32)
        def _(r):
            at = pl.ds(pl.multiple_of(r * 32, 32), 32)
            mix = mixed(c, 0, r)
            og_ref[at, cols] = mix[:, :LANES]
            ou_ref[at, cols] = mix[:, LANES:]

    for c in range(CHUNKS):
        cols = columns(c, 1 - half(c, v))
        over(c).wait_recv()
        og_ref[:, cols] = mix_r[c, :, :LANES]
        ou_ref[:, cols] = mix_r[c, :, LANES:]
    for c in range(CHUNKS):
        over(c).wait_send()


def local(tokens, hidden_grad, gate_weight, up_weight, counts):
    vmem = pl.BlockSpec(memory_space=pltpu.VMEM)
    dma = pltpu.SemaphoreType.DMA
    bf16, f32 = jnp.bfloat16, jnp.float32
    mix_gate, mix_up, alpha = pl.pallas_call(
        kernel,
        out_shape=(
            jax.ShapeDtypeStruct((ROWS, 4 * LANES), f32),
            jax.ShapeDtypeStruct((ROWS, 4 * LANES), f32),
            jax.ShapeDtypeStruct((1, N_DOM), f32),
        ),
        in_specs=[vmem] * 4 + [pl.BlockSpec(memory_space=pltpu.SMEM)],
        out_specs=(vmem,) * 3,
        scratch_shapes=[
            pltpu.VMEM((SHARED, CHUNKS, TOKENS, LANES), bf16),
            pltpu.VMEM((SHARED, TOKENS, D), bf16),
            pltpu.VMEM((SHARED, D, TOKENS), bf16),
            pltpu.VMEM((CHUNKS, 2, SIDE, SIDE, ROWS, LANES), bf16),
            pltpu.VMEM((SHARED, CHUNKS, 8, 2 * ROWS, 2 * LANES), bf16),
            pltpu.VMEM((CHUNKS, N_DOM, 2 * ROWS, 2 * LANES), bf16),
            pltpu.VMEM((TOKENS, 2 * LANES), bf16),
            pltpu.VMEM((2 * ROWS, 2 * LANES), f32),
            pltpu.VMEM((N_DOM, 1, 2 * LANES), f32),
            pltpu.VMEM((2 * N_DOM, 1, LANES), f32),
            pltpu.VMEM((8, LANES), f32),
            pltpu.VMEM((8, LANES), f32),
            pltpu.VMEM((N_DOM, 8, LANES), f32),
            pltpu.VMEM((N_FSDP, 8, LANES), f32),
            pltpu.VMEM((CHUNKS, ROWS, 2 * LANES), f32),
            pltpu.VMEM((CHUNKS, ROWS, 2 * LANES), f32),
            dma((SHARED, 7, PIECES)), dma((SHARED, 7, PIECES)), dma((SHARED, 8, PIECES)), dma((SHARED, 8, PIECES)),
            dma((1,)), dma((1,)), dma((CHUNKS,)), dma((CHUNKS,)),
            dma((CHUNKS, 2, 4)), dma((CHUNKS, 2, 4)), dma((CHUNKS, 4)), dma((CHUNKS, 4)),
            dma((SHARED, CHUNKS, 8)), dma((SHARED, CHUNKS, 8)),
            dma((N_DOM,)), dma((N_DOM,)), dma((N_FSDP,)), dma((N_FSDP,)), dma((CHUNKS,)), dma((CHUNKS,)),
        ],
        compiler_params=pltpu.CompilerParams(
            collective_id=0, has_side_effects=True, vmem_limit_bytes=60 * 2**20
        ),
        cost_estimate=pl.CostEstimate(flops=13 * 10**9, bytes_accessed=4 * 10**6, transcendentals=400000),
    )(tokens, hidden_grad, gate_weight, up_weight, counts)
    return mix_gate, mix_up, alpha.reshape(N_DOM)


def solution(mesh):
    return jax.shard_map(
        local,
        mesh=mesh,
        in_specs=(
            P("dom", "fsdp", None),
            P("dom", None, "fsdp"),
            P("dom", "fsdp"),
            P("dom", "fsdp"),
            P(),
        ),
        out_specs=(P("dom", "fsdp"), P("dom", "fsdp"), P()),
        check_vma=False,
    )
```
